256 devices in a mesh: slab: 64 (over x_hi, z, y), mode: 4 (over x_lo, core).
Axes of the slice: x: 4 (x_hi: 2, x_lo: 2; x = x_hi * 2 + x_lo), y: 4, z: 8, core: 2. Of those that a mesh axis runs over, the one named last changes fastest.
Arguments:
- subspace: float32 [192, 3, 128, 8, 128], P('mode', None, 'slab'), may hold values from -32 to 32
- modulus: float32 [128, 8, 128], P('slab'), may hold values from 0.3 to 3
- mass: float32 [128, 8, 128], P('slab'), may hold values from 0.3 to 3
- support: int32 [128, 8, 128], P('slab'), may hold values 0 or 1
- stiffness: float32 [24, 24], replicated, may hold values from -0.04 to 1.5, as said below
Outputs:
- filtered: float32 [192, 3, 128, 8, 128], P('mode', None, 'slab')
- stiffness_gram: float32 [192, 192], P('mode')
- mass_gram: float32 [192, 192], P('mode')
The draws below stay inside these ranges and needn't reach their ends.
Inputs may be any that keep to these rules, and one draw needn't show every extreme that they name: `stiffness`: Symmetric; the diagonal lies in 1 to 1.5 and the magnitudes off the diagonal of each row sum to less than 0.9.
All inputs are finite; a program needn't handle non-finite values. No bound on the sum of `support` on one device may be relied on, other than what follows from the above.
Results may differ from the reference program's by a relative error of at most 0.0001.
Values sent between devices are 32-bit elements; how exact they have to be, the bound alone decides.
No kernel may reach another device: no remote copies, remote signals or barrier semaphores. Data moves between devices by JAX's collectives and lax.ppermute only.
A program may use at most 128 MiB of HBM per device.

```python
import math
import jax
import jax.numpy as jnp
from jax import lax

MODES = 192
DEGREE = 4
NY = 8
NZ = 128
NX = 128
DOFS = 393216


def draw_subspace(key, part):
    key = jax.random.fold_in(key, 11)
    base_key, mode_key = jax.random.split(key, 2)
    base = jnp.clip(jax.random.normal(base_key, (MODES, 3, NX, NY, NZ), jnp.float32), -5.0, 5.0)
    mode_scale = jnp.exp(jax.random.uniform(mode_key, (MODES, 1, 1, 1, 1), jnp.float32, -0.7, 0.7))
    return base * mode_scale


def draw_stiffness(key, part):
    key = jax.random.fold_in(key, 23)
    off_key, diag_key = jax.random.split(key)
    raw = jax.random.uniform(off_key, (24, 24), jnp.float32, -1.0, 1.0)
    symmetric = (raw + raw.T) * 0.5 * 0.039
    diagonal = jax.random.uniform(diag_key, (24,), jnp.float32, 1.0, 1.5)
    identity = jnp.eye(24, dtype=jnp.float32)
    return symmetric * (1.0 - identity) + identity * diagonal[None, :]


def touch_ends(result, stream_key, smallest, top_value):
    longest = result.shape.index(max(result.shape))
    spots = []
    for shift in (0, 1):
        where = [jax.random.randint(jax.random.fold_in(stream_key, axis), (), 0, length) for axis, length in enumerate(result.shape)]
        where[longest] = (where[longest] + shift) % result.shape[longest]
        spots.append(tuple(where))
    return result.at[spots[0]].set(smallest).at[spots[1]].set(top_value)


def levels(rng, shape, cuts, smallest, top_value):
    level, own = 1.0, jax.random.fold_in(rng, 6)
    for axis_at, parts in cuts:
        steps = jnp.exp(jax.random.uniform(jax.random.fold_in(own, axis_at), (parts,), jnp.float32, smallest / len(cuts), top_value / len(cuts)))
        level = level * jnp.repeat(steps, shape[axis_at] // parts).reshape([-1 if axis == axis_at else 1 for axis in range(len(shape))])
    return level


def setup_inputs(seed: int = 0) -> dict:
    splits = jax.random.split(jax.random.key(seed), 6)
    return {
        "subspace": draw_subspace(jax.random.fold_in(splits[5], 71), 0),
        "modulus": jnp.clip(jnp.exp(math.log(3.0) - 2.3025851 * jax.random.uniform(splits[1], (NX, NY, NZ), jnp.float32) ** levels(splits[1], (NX, NY, NZ), ((0, 64),), -0.2, 0.2)), 0.3, 3.0),
        "mass": jnp.clip(jnp.exp(math.log(3.0) - 2.3025851 * jax.random.uniform(splits[2], (NX, NY, NZ), jnp.float32) ** levels(splits[2], (NX, NY, NZ), ((0, 64),), -0.2, 0.2)), 0.3, 3.0),
        "support": touch_ends((jax.random.randint(splits[3], (NX, NY, NZ), 0, 8) < 1).astype(jnp.int32), jax.random.fold_in(splits[3], 1), 0, 1),
        "stiffness": draw_stiffness(jax.random.fold_in(splits[5], 71), 0),
    }


corner_offsets = ((0, 0, 0), (0, 0, 1), (0, 1, 0), (0, 1, 1), (1, 0, 0), (1, 0, 1), (1, 1, 0), (1, 1, 1))
center_value = 110.0
half_width = 90.0
highest = lax.Precision.HIGHEST


def lift(array, shift_x, shift_y, shift_z):
    shape = array.shape
    padded = jnp.pad(array, ((0, 0), (0, 0), (shift_x, 0), (shift_y, 0), (shift_z, 0)))
    return padded[:, :, :shape[2], :shape[3], :shape[4]]


def element_nodes(field, effective, stiffness):
    group = field.shape[0]
    extent_x, extent_y, extent_z = field.shape[2], field.shape[3], field.shape[4]
    padded = jnp.pad(field, ((0, 0), (0, 0), (0, 1), (0, 1), (0, 1)))
    corners = [padded[:, :, sx:sx + extent_x, sy:sy + extent_y, sz:sz + extent_z] for (sx, sy, sz) in corner_offsets]
    local = jnp.stack(corners, 0).transpose(0, 2, 1, 3, 4, 5).reshape((24, group, extent_x, extent_y, extent_z))
    force = jnp.einsum('rs,sgxyz->rgxyz', stiffness, local, precision=highest) * effective[None, None]
    force = force.reshape((8, 3, group, extent_x, extent_y, extent_z))
    total = lift(force[0], 0, 0, 0)
    for index in range(1, 8):
        shift_x, shift_y, shift_z = corner_offsets[index]
        total = total + lift(force[index], shift_x, shift_y, shift_z)
    return total.transpose(1, 0, 2, 3, 4)


def reference(subspace, modulus, mass, support, stiffness):
    free = (1 - support).astype(jnp.float32)[None, None]
    weights = mass[None, None]
    plane_index = lax.broadcasted_iota(jnp.int32, modulus.shape, 0)
    row_index = lax.broadcasted_iota(jnp.int32, modulus.shape, 1)
    depth_index = lax.broadcasted_iota(jnp.int32, modulus.shape, 2)
    valid = (plane_index < NX - 1) & (row_index < NY - 1) & (depth_index < NZ - 1)
    effective = jnp.where(valid, modulus, jnp.zeros_like(modulus))
    group = math.gcd(MODES, 16)

    def operate(field):
        return free * element_nodes(field, effective, stiffness)

    def filter_group(block):
        previous = free * block
        current = (operate(previous) / weights - center_value * previous) / half_width
        for step in range(DEGREE - 1):
            following = 2.0 * (operate(current) / weights - center_value * current) / half_width - previous
            previous, current = current, following
        return current, operate(current)

    blocks = subspace.reshape((MODES // group, group, 3, NX, NY, NZ))
    filtered, stiffened = lax.map(filter_group, blocks)
    filtered = filtered.reshape((MODES, 3, NX, NY, NZ))
    stiffened = stiffened.reshape((MODES, 3, NX, NY, NZ))
    stiffness_gram = jnp.einsum('acxyz,bcxyz->ab', stiffened, filtered, precision=highest) / DOFS
    mass_gram = jnp.einsum('acxyz,bcxyz->ab', filtered * weights, filtered, precision=highest) / DOFS
    return filtered, stiffness_gram, mass_gram
```

```python
from functools import partial

import jax
import jax.numpy as jnp
from jax import lax
from jax.experimental import pallas as pl
from jax.experimental.pallas import tpu as pltpu
from jax.sharding import Mesh, PartitionSpec as P

CENTER = 110.0
HALF = 90.0
SLAB = ("xh", "z", "y")
MODE = ("xl", "core")
STEPS = (0, 1, -1)
VMEM_LIMIT = 48 * 1024 * 1024


def spec(shape):
    return jax.ShapeDtypeStruct(shape, jnp.float32)


def own_index(dz, q, e, dy, c, p):
    return ((((STEPS.index(dz) * 2 + q) * 3 + e) * 3 + STEPS.index(dy)) * 3 + c) * 2 + p


def halo_index(dz, side, e, dy, c):
    return (((STEPS.index(dz) * 2 + side) * 3 + e) * 3 + STEPS.index(dy)) * 3 + c


def rolled(x, by, axis):
    by = by % x.shape[axis]
    return x if by == 0 else pltpu.roll(x, by, axis)


def coefficient_kernel(stiff_ref, layers_ref, own_ref, halo_ref):
    turned = {}
    for layer in range(3):
        for b in range(2):
            for d in range(2):
                turned[layer, b, d] = rolled(rolled(layers_ref[layer], b, 0), d, 1)
    for p in range(2):
        for q in range(-1, 3):
            dx = q - p
            if abs(dx) > 1:
                continue
            for dy in STEPS:
                for dz in STEPS:
                    corners = [
                        (a, b, d)
                        for a in range(2)
                        for b in range(2)
                        for d in range(2)
                        if 0 <= a + dx <= 1 and 0 <= b + dy <= 1 and 0 <= d + dz <= 1
                    ]
                    for c in range(3):
                        for e in range(3):
                            total = None
                            for a, b, d in corners:
                                row = 3 * (4 * a + 2 * b + d) + c
                                col = 3 * (4 * (a + dx) + 2 * (b + dy) + d + dz) + e
                                term = stiff_ref[row, col] * turned[p - a + 1, b + dy, d]
                                total = term if total is None else total + term
                            if 0 <= q <= 1:
                                own_ref[own_index(dz, q, e, dy, c, p)] = total
                            else:
                                halo_ref[halo_index(dz, 0 if q < 0 else 1, e, dy, c)] = total


def coefficients(stiffness, layers):
    rows, depth = layers.shape[1:]
    return pl.pallas_call(
        coefficient_kernel,
        in_specs=[pl.BlockSpec(memory_space=pltpu.SMEM), pl.BlockSpec(memory_space=pltpu.VMEM)],
        out_specs=[pl.BlockSpec(memory_space=pltpu.VMEM)] * 2,
        out_shape=[spec((324, rows, depth)), spec((162, rows, depth))],
        compiler_params=pltpu.CompilerParams(vmem_limit_bytes=VMEM_LIMIT),
    )(stiffness, layers)


PAIR = 2


def gathered(acc):
    return acc[0] + rolled(acc[1], -1, 0) + rolled(acc[2], 1, 0)


def own_kernel(low_ref, high_ref, coef_ref, part_ref):
    planes = (low_ref, high_ref)

    def pair(i, _):
        base = i * (3 * PAIR)
        acc = {}
        for dz in STEPS:
            for q in range(2):
                for e in range(3):
                    fields = [rolled(planes[q][base + 3 * u + e], -dz, 1) for u in range(PAIR)]
                    for s, dy in enumerate(STEPS):
                        for c in range(3):
                            for p in range(2):
                                coef = coef_ref[own_index(dz, q, e, dy, c, p)]
                                for u in range(PAIR):
                                    term = coef * fields[u]
                                    key = (u, c, p, s)
                                    acc[key] = acc[key] + term if key in acc else term
        for u in range(PAIR):
            for c in range(3):
                for p in range(2):
                    part_ref[base + 3 * u + c, p] = gathered([acc[u, c, p, s] for s in range(3)])
        return 0

    lax.fori_loop(0, low_ref.shape[0] // (3 * PAIR), pair, 0)


def block(shape):
    return pl.BlockSpec(shape, lambda i: (i,) + (0,) * (len(shape) - 1))


def whole(shape):
    return pl.BlockSpec(shape, lambda i: (0,) * len(shape))


def cost(flops, nbytes):
    return pl.CostEstimate(flops=flops, bytes_accessed=nbytes, transcendentals=0)


GRID = 4


def own_part(low, high, coef):
    count, rows, depth = low.shape
    tile = count // GRID
    return pl.pallas_call(
        own_kernel,
        grid=(GRID,),
        in_specs=[block((tile, rows, depth)), block((tile, rows, depth)), whole(coef.shape)],
        out_specs=block((tile, 2, rows, depth)),
        out_shape=spec((count, 2, rows, depth)),
        cost_estimate=cost(2 * 108 * count * rows * depth, 4 * (4 * count + 324) * rows * depth),
        compiler_params=pltpu.CompilerParams(vmem_limit_bytes=VMEM_LIMIT),
    )(low, high, coef)


def halo_body(lower_ref, upper_ref, part_ref, coef_ref, base):
    sides = (lower_ref, upper_ref)
    acc = {}
    for dz in STEPS:
        for side in range(2):
            for e in range(3):
                fields = [rolled(sides[side][base + 3 * u + e], -dz, 1) for u in range(PAIR)]
                for s, dy in enumerate(STEPS):
                    for c in range(3):
                        coef = coef_ref[halo_index(dz, side, e, dy, c)]
                        for u in range(PAIR):
                            term = coef * fields[u]
                            key = (u, c, side, s)
                            acc[key] = acc[key] + term if key in acc else term
    force = {}
    for u in range(PAIR):
        for c in range(3):
            for p in range(2):
                near = gathered([acc[u, c, p, s] for s in range(3)])
                force[u, c, p] = part_ref[base + 3 * u + c, p] + near
    return force


def step_kernel(first, last, *refs):
    lower_ref, upper_ref, part_ref, coef_ref, scale_ref, low_ref, high_ref = refs[:7]
    if first:
        outs = refs[7:]
    else:
        before = refs[7:9]
        outs = refs[9:]
    current = (low_ref, high_ref)

    def pair(i, _):
        base = i * (3 * PAIR)
        force = halo_body(lower_ref, upper_ref, part_ref, coef_ref, base)
        for u in range(PAIR):
            for c in range(3):
                for p in range(2):
                    at = base + 3 * u + c
                    value = scale_ref[p] * force[u, c, p] - (CENTER / HALF) * current[p][at]
                    if not first:
                        value = 2.0 * value - before[p][at]
                    outs[p][at] = value
                    if last:
                        outs[2][at, p] = value
        return 0

    lax.fori_loop(0, low_ref.shape[0] // (3 * PAIR), pair, 0)


def step(first, last, lower, upper, part, coef, scale, current, before):
    count, rows, depth = lower.shape
    tile = count // GRID
    plane = block((tile, rows, depth))
    both = block((tile, 2, rows, depth))
    args = [lower, upper, part, coef, scale, *current] + ([] if first else list(before))
    return pl.pallas_call(
        partial(step_kernel, first, last),
        grid=(GRID,),
        in_specs=[plane, plane, both, whole(coef.shape), whole(scale.shape)]
        + [plane] * (len(args) - 5),
        out_specs=[plane, plane] + ([both] if last else []),
        out_shape=[spec(lower.shape)] * 2 + ([spec((count, 2, rows, depth))] if last else []),
        cost_estimate=cost(2 * 54 * count * rows * depth, 4 * (10 * count + 162) * rows * depth),
        compiler_params=pltpu.CompilerParams(vmem_limit_bytes=VMEM_LIMIT),
    )(*args)


def force_kernel(lower_ref, upper_ref, part_ref, coef_ref, free_ref, out_ref):
    def pair(i, _):
        base = i * (3 * PAIR)
        force = halo_body(lower_ref, upper_ref, part_ref, coef_ref, base)
        for u in range(PAIR):
            for c in range(3):
                for p in range(2):
                    out_ref[base + 3 * u + c, p] = free_ref[p] * force[u, c, p]
        return 0

    lax.fori_loop(0, lower_ref.shape[0] // (3 * PAIR), pair, 0)


def forced(lower, upper, part, coef, free):
    count, rows, depth = lower.shape
    tile = count // GRID
    plane = block((tile, rows, depth))
    both = block((tile, 2, rows, depth))
    return pl.pallas_call(
        force_kernel,
        grid=(GRID,),
        in_specs=[plane, plane, both, whole(coef.shape), whole(free.shape)],
        out_specs=both,
        out_shape=spec((count, 2, rows, depth)),
        cost_estimate=cost(2 * 54 * count * rows * depth, 4 * (6 * count + 162) * rows * depth),
        compiler_params=pltpu.CompilerParams(vmem_limit_bytes=VMEM_LIMIT),
    )(lower, upper, part, coef, free)


def split(x):
    top = x.astype(jnp.bfloat16)
    return top, (x - top.astype(jnp.float32)).astype(jnp.bfloat16)


def dot_t(a, b):
    return lax.dot_general(a, b, (((1,), (1,)), ((), ())), preferred_element_type=jnp.float32)


def gram_kernel(stiff_ref, mass_ref, *refs):
    fields, out_ref = refs[:4], refs[4]
    modes = out_ref.shape[1]
    nodes = mass_ref.shape[0]
    comps = stiff_ref.shape[0] // (modes * nodes)

    out_ref[...] = jnp.zeros_like(out_ref)

    def slice_at(ref, c, n):
        return ref[pl.ds(c * nodes + n, modes, stride=comps * nodes), :]

    def some(n, _):
        weight = mass_ref[pl.ds(n, 1), :]
        for c in range(comps):
            own = slice_at(fields[0], c, n)
            left = jnp.concatenate([slice_at(stiff_ref, c, n), own * weight], 0)
            left_top, left_rest = split(left)
            for r in range(4):
                top, rest = split(own if r == 0 else slice_at(fields[r], c, n))
                out = dot_t(left_top, top) + (dot_t(left_top, rest) + dot_t(left_rest, top))
                out_ref[r] = out_ref[r] + jnp.concatenate([out[:modes], out[modes:]], 1)
        return 0

    lax.fori_loop(0, nodes, some, 0)


def gram(stiff, mass, fields, modes):
    return pl.pallas_call(
        gram_kernel,
        out_shape=spec((4, modes, 2 * modes)),
        compiler_params=pltpu.CompilerParams(vmem_limit_bytes=VMEM_LIMIT),
    )(stiff, mass, *fields)


def total_over(x, axis):
    count = lax.axis_size(axis)
    parts = [
        lax.ppermute(x, axis, [(i, (i + k) % count) for i in range(count)]) for k in range(1, count)
    ]
    for part in parts:
        x = x + part
    return x


def body(subspace, modulus, mass, support, stiffness):
    modes, comps, planes, rows, depth = subspace.shape
    slabs = lax.axis_size(SLAB)
    up = [(i, (i + 1) % slabs) for i in range(slabs)]
    down = [((i + 1) % slabs, i) for i in range(slabs)]
    lower_layer = lax.ppermute(modulus[planes - 1 :], SLAB, up)
    free = (1 - support).astype(jnp.float32)

    def masked(p):
        return (free[p] * subspace[:, :, p]).reshape(modes * comps, rows, depth)

    current = (masked(0), masked(1))
    layers = jnp.concatenate([lower_layer, modulus], 0)
    plane_index = (
        lax.axis_index(SLAB) * planes - 1 + lax.broadcasted_iota(jnp.int32, layers.shape, 0)
    )
    row_index = lax.broadcasted_iota(jnp.int32, layers.shape, 1)
    depth_index = lax.broadcasted_iota(jnp.int32, layers.shape, 2)
    valid = (
        (plane_index >= 0)
        & (plane_index < planes * slabs - 1)
        & (row_index < rows - 1)
        & (depth_index < depth - 1)
    )
    layers = jnp.where(valid, layers, jnp.zeros_like(layers))
    own_coef, halo_coef = coefficients(stiffness, layers)
    scale = free / (mass * HALF)

    before = None
    filtered = None
    for k in range(4):
        lower = lax.ppermute(current[1], SLAB, up)
        upper = lax.ppermute(current[0], SLAB, down)
        part = own_part(*current, own_coef)
        result = step(k == 0, k == 3, lower, upper, part, halo_coef, scale, current, before)
        before, current = current, result[:2]
        if k == 3:
            filtered = result[2]
    swap = [(0, 1), (1, 0)]
    lower = lax.ppermute(current[1], SLAB, up)
    upper = lax.ppermute(current[0], SLAB, down)
    by_x = lax.ppermute(filtered, "xl", swap)
    by_core = lax.ppermute(filtered, "core", swap)
    part = own_part(*current, own_coef)
    by_both = lax.ppermute(by_x, "core", swap)
    stiffened = forced(lower, upper, part, halo_coef, free)
    flat = (-1, depth)
    fields = [a.reshape(flat) for a in (filtered, by_core, by_x, by_both)]
    grams = gram(stiffened.reshape(flat), mass.reshape(flat), fields, modes)
    for axis in SLAB[::-1]:
        grams = total_over(grams, axis)
    grams = grams / (float(comps) * planes * slabs * rows * depth)
    swapped = lax.axis_index("core") == 1
    grams = jnp.where(swapped, grams[jnp.array([1, 0, 3, 2])], grams)
    swapped = lax.axis_index("xl") == 1
    grams = jnp.where(swapped, grams[jnp.array([2, 3, 0, 1])], grams)
    grams = grams.reshape(4, modes, 2, modes).transpose(2, 1, 0, 3).reshape(2, modes, 4 * modes)
    return filtered.reshape(modes, comps, planes, rows, depth), grams[0], grams[1]


def solution(mesh):
    finer = Mesh(mesh.devices.reshape(2, 8, 4, 2, 2), SLAB + MODE)
    placed = (
        P(MODE, None, SLAB, None, None),
        P(SLAB, None, None),
        P(SLAB, None, None),
        P(SLAB, None, None),
        P(),
    )
    return jax.shard_map(
        body,
        mesh=finer,
        in_specs=placed,
        out_specs=(P(MODE, None, SLAB, None, None), P(MODE, None), P(MODE, None)),
        check_vma=False,
    )
```

```python
from functools import partial

import jax
import jax.numpy as jnp
from jax import lax
from jax.experimental import pallas as pl
from jax.experimental.pallas import tpu as pltpu
from jax.sharding import Mesh, PartitionSpec as P

CENTER = 110.0
HALF = 90.0
SLAB = ("xh", "z", "y")
MODE = ("xl", "core")
STEPS = (0, 1, -1)
VMEM_LIMIT = 48 * 1024 * 1024


def spec(shape):
    return jax.ShapeDtypeStruct(shape, jnp.float32)


def own_index(dz, q, e, dy, c, p):
    return ((((STEPS.index(dz) * 2 + q) * 3 + e) * 3 + STEPS.index(dy)) * 3 + c) * 2 + p


def halo_index(dz, side, e, dy, c):
    return (((STEPS.index(dz) * 2 + side) * 3 + e) * 3 + STEPS.index(dy)) * 3 + c


def rolled(x, by, axis):
    by = by % x.shape[axis]
    return x if by == 0 else pltpu.roll(x, by, axis)


def coefficient_kernel(stiff_ref, layers_ref, own_ref, halo_ref):
    turned = {}
    for layer in range(3):
        for b in range(2):
            for d in range(2):
                turned[layer, b, d] = rolled(rolled(layers_ref[layer], b, 0), d, 1)
    for p in range(2):
        for q in range(-1, 3):
            dx = q - p
            if abs(dx) > 1:
                continue
            for dy in STEPS:
                for dz in STEPS:
                    corners = [
                        (a, b, d)
                        for a in range(2)
                        for b in range(2)
                        for d in range(2)
                        if 0 <= a + dx <= 1 and 0 <= b + dy <= 1 and 0 <= d + dz <= 1
                    ]
                    for c in range(3):
                        for e in range(3):
                            total = None
                            for a, b, d in corners:
                                row = 3 * (4 * a + 2 * b + d) + c
                                col = 3 * (4 * (a + dx) + 2 * (b + dy) + d + dz) + e
                                term = stiff_ref[row, col] * turned[p - a + 1, b + dy, d]
                                total = term if total is None else total + term
                            if 0 <= q <= 1:
                                own_ref[own_index(dz, q, e, dy, c, p)] = total
                            else:
                                halo_ref[halo_index(dz, 0 if q < 0 else 1, e, dy, c)] = total


def coefficients(stiffness, layers):
    rows, depth = layers.shape[1:]
    return pl.pallas_call(
        coefficient_kernel,
        in_specs=[pl.BlockSpec(memory_space=pltpu.SMEM), pl.BlockSpec(memory_space=pltpu.VMEM)],
        out_specs=[pl.BlockSpec(memory_space=pltpu.VMEM)] * 2,
        out_shape=[spec((324, rows, depth)), spec((162, rows, depth))],
        compiler_params=pltpu.CompilerParams(vmem_limit_bytes=VMEM_LIMIT),
    )(stiffness, layers)


OWN_MODES = 2
HALO_MODES = 4
IN_VMEM = pl.BlockSpec(memory_space=pltpu.VMEM)
ANYWHERE = pl.BlockSpec(memory_space=pl.ANY)


def cost(flops, nbytes):
    return pl.CostEstimate(flops=flops, bytes_accessed=nbytes, transcendentals=0)


def compiled():
    return pltpu.CompilerParams(vmem_limit_bytes=VMEM_LIMIT)


def gathered(acc):
    return acc[0] + rolled(acc[1], -1, 0) + rolled(acc[2], 1, 0)


def added(acc, key, term):
    acc[key] = acc[key] + term if key in acc else term


def own_kernel(shift, count, *refs):
    low_ref, high_ref, coef_ref, scale_ref = refs[:4]
    before, part_ref = refs[4:-1], refs[-1]
    planes = (low_ref, high_ref)

    def some(i, _):
        base = i * (3 * OWN_MODES)
        acc = {}
        for dz in STEPS:
            for q in range(2):
                for e in range(3):
                    fields = [rolled(planes[q][base + 3 * u + e], -dz, 1) for u in range(OWN_MODES)]
                    for s, dy in enumerate(STEPS):
                        for c in range(3):
                            for p in range(2):
                                coef = coef_ref[own_index(dz, q, e, dy, c, p)]
                                for u in range(OWN_MODES):
                                    added(acc, (u, c, p, s), coef * fields[u])
        for u in range(OWN_MODES):
            for c in range(3):
                at = base + 3 * u + c
                for p in range(2):
                    value = scale_ref[p] * gathered([acc[u, c, p, s] for s in range(3)])
                    if shift:
                        value = value - shift * planes[p][at]
                    if before:
                        value = value - before[p][at]
                    part_ref[at, p] = value
        return 0

    lax.fori_loop(0, count // (3 * OWN_MODES), some, 0)


def own_part(shift, current, coef, scale, before):
    count, rows, depth = current[0].shape
    args = (*current, coef, scale, *before)
    return pl.pallas_call(
        partial(own_kernel, shift, count),
        in_specs=[IN_VMEM] * len(args),
        out_specs=IN_VMEM,
        out_shape=spec((count, 2, rows, depth)),
        cost_estimate=cost(2 * 108 * count * rows * depth, 16 << 20),
        compiler_params=compiled(),
    )(*args)


def halo_kernel(count, lower_ref, upper_ref, part_ref, coef_ref, scale_ref, *outs):
    sides = (lower_ref, upper_ref)

    def some(i, _):
        base = i * (3 * HALO_MODES)
        for p in range(2):
            acc = {}
            for dz in STEPS:
                for e in range(3):
                    fields = [rolled(sides[p][base + 3 * u + e], -dz, 1) for u in range(HALO_MODES)]
                    for s, dy in enumerate(STEPS):
                        for c in range(3):
                            coef = coef_ref[halo_index(dz, p, e, dy, c)]
                            for u in range(HALO_MODES):
                                added(acc, (u, c, s), coef * fields[u])
            for u in range(HALO_MODES):
                for c in range(3):
                    at = base + 3 * u + c
                    near = gathered([acc[u, c, s] for s in range(3)])
                    value = part_ref[at, p] + scale_ref[p] * near
                    if len(outs) > 1:
                        outs[p][at] = value
                    if len(outs) != 2:
                        outs[-1][at, p] = value
        return 0

    lax.fori_loop(0, count // (3 * HALO_MODES), some, 0)


def with_halo(lower, upper, part, coef, scale, outs, passed=None):
    count, rows, depth = lower.shape
    plane, both = spec(lower.shape), spec(part.shape)
    shapes = {1: [both], 2: [plane] * 2, 3: [plane, plane, both]}[outs]
    args = [lower, upper, part, coef, scale]
    specs, out_specs = [IN_VMEM] * 5, [IN_VMEM] * outs
    kernel = partial(halo_kernel, count)
    aliases = {}
    if passed is not None:
        args, specs = args + [passed], specs + [ANYWHERE]
        shapes, out_specs = shapes + [spec(passed.shape)], out_specs + [ANYWHERE]
        aliases = {5: outs}

        def kernel(*refs):
            halo_kernel(count, *refs[:5], *refs[6:-1])

    return pl.pallas_call(
        kernel,
        in_specs=specs,
        out_specs=out_specs,
        out_shape=shapes,
        input_output_aliases=aliases,
        cost_estimate=cost(2 * 54 * count * rows * depth, 9 << 20),
        compiler_params=compiled(),
    )(*args)


def split(x):
    top = x.astype(jnp.bfloat16)
    return top, (x - top.astype(jnp.float32)).astype(jnp.bfloat16)


def dot_t(a, b):
    return lax.dot_general(a, b, (((1,), (1,)), ((), ())), preferred_element_type=jnp.float32)


def gram_kernel(factor, place_ref, stiff_ref, mass_ref, *refs):
    fields, out_ref = refs[:4], refs[4]
    left_top, left_rest, top, rest, turned = refs[5:]
    modes = out_ref.shape[0] // 2
    nodes, depth = mass_ref.shape
    comps = stiff_ref.shape[0] // (modes * nodes)

    def some(n, _):
        weight = mass_ref[pl.ds(n, 1), :]
        for c in range(comps):
            row = c * nodes + n
            at = pl.ds(pl.multiple_of(row * depth, depth), depth)
            for r in range(4):
                value = fields[r][pl.ds(row, modes, stride=comps * nodes), :]
                rows = pl.ds(r * modes, modes)
                top[rows, at], rest[rows, at] = split(value)
                if r == 0:
                    rows = pl.ds(modes, modes)
                    left_top[rows, at], left_rest[rows, at] = split(value * weight)
            value = stiff_ref[pl.ds(row, modes, stride=comps * nodes), :]
            rows = pl.ds(0, modes)
            left_top[rows, at], left_rest[rows, at] = split(value)
        return 0

    lax.fori_loop(0, nodes, some, 0)
    total = dot_t(top[...], left_top[...])
    total = total + dot_t(rest[...], left_top[...])
    total = (total + dot_t(top[...], left_rest[...])) * factor
    for r in range(4):
        at = pl.ds(pl.multiple_of(place_ref[r] * modes, modes), modes)
        turned[at, :] = total[r * modes : (r + 1) * modes]
    out_ref[...] = turned[...].T


def gram(factor, place, stiff, mass, fields, modes):
    wide = stiff.size // modes
    return pl.pallas_call(
        partial(gram_kernel, factor),
        in_specs=[pl.BlockSpec(memory_space=pltpu.SMEM)] + [IN_VMEM] * 6,
        out_specs=IN_VMEM,
        out_shape=spec((2 * modes, 4 * modes)),
        scratch_shapes=[
            pltpu.VMEM((2 * modes, wide), jnp.bfloat16),
            pltpu.VMEM((2 * modes, wide), jnp.bfloat16),
            pltpu.VMEM((4 * modes, wide), jnp.bfloat16),
            pltpu.VMEM((4 * modes, wide), jnp.bfloat16),
            pltpu.VMEM((4 * modes, 2 * modes), jnp.float32),
        ],
        compiler_params=compiled(),
    )(place, stiff, mass, *fields)


def total_over(x, axes, groups):
    above, count, below = groups
    parts = []
    for k in range(1, count):
        pairs = [
            ((i * count + j) * below + l, (i * count + (j + k) % count) * below + l)
            for i in range(above)
            for j in range(count)
            for l in range(below)
        ]
        parts.append(lax.ppermute(x, axes, pairs))
    for part in parts:
        x = x + part
    return x


def body(subspace, modulus, mass, support, stiffness):
    modes, comps, planes, rows, depth = subspace.shape
    slabs = lax.axis_size(SLAB)
    up = [(i, (i + 1) % slabs) for i in range(slabs)]
    down = [((i + 1) % slabs, i) for i in range(slabs)]
    lower_layer = lax.ppermute(modulus[planes - 1 :], SLAB, up)
    free = (1 - support).astype(jnp.float32)

    def masked(p):
        return (free[p] * subspace[:, :, p]).reshape(modes * comps, rows, depth)

    current = (masked(0), masked(1))
    layers = jnp.concatenate([lower_layer, modulus], 0)
    plane_index = (
        lax.axis_index(SLAB) * planes - 1 + lax.broadcasted_iota(jnp.int32, layers.shape, 0)
    )
    row_index = lax.broadcasted_iota(jnp.int32, layers.shape, 1)
    depth_index = lax.broadcasted_iota(jnp.int32, layers.shape, 2)
    valid = (
        (plane_index >= 0)
        & (plane_index < planes * slabs - 1)
        & (row_index < rows - 1)
        & (depth_index < depth - 1)
    )
    layers = jnp.where(valid, layers, jnp.zeros_like(layers))
    own_coef, halo_coef = coefficients(stiffness, layers)
    scale = free / (mass * HALF)

    before = ()
    for k in range(4):
        times = 1.0 if k == 0 else 2.0
        lower = lax.ppermute(current[1], SLAB, up)
        upper = lax.ppermute(current[0], SLAB, down)
        part = own_part(times * CENTER / HALF, current, own_coef, times * scale, before)
        result = with_halo(lower, upper, part, halo_coef, times * scale, 3 if k == 3 else 2)
        before, current = current, tuple(result[:2])
    filtered = result[2]
    swap = [(0, 1), (1, 0)]
    lower = lax.ppermute(current[1], SLAB, up)
    upper = lax.ppermute(current[0], SLAB, down)
    by_x = lax.ppermute(filtered, "xl", swap)
    by_core = lax.ppermute(filtered, "core", swap)
    part = own_part(0.0, current, own_coef, free, ())
    stiffened, by_x = with_halo(lower, upper, part, halo_coef, free, 1, by_x)
    by_both = lax.ppermute(by_x, "core", swap)
    flat = (-1, depth)
    fields = [a.reshape(flat) for a in (filtered, by_core, by_x, by_both)]
    me = lax.axis_index(MODE)
    place = jnp.stack([me ^ r for r in range(4)]).astype(jnp.int32)
    factor = 1.0 / (float(comps) * planes * slabs * rows * depth)
    grams = gram(factor, place, stiffened.reshape(flat), mass.reshape(flat), fields, modes)
    for groups in ((16, 4, 1), (4, 4, 4), (2, 2, 16), (1, 2, 32)):
        grams = total_over(grams, SLAB, groups)
    return filtered.reshape(subspace.shape), grams[:modes], grams[modes:]


def solution(mesh):
    finer = Mesh(mesh.devices.reshape(2, 8, 4, 2, 2), SLAB + MODE)
    placed = (
        P(MODE, None, SLAB, None, None),
        P(SLAB, None, None),
        P(SLAB, None, None),
        P(SLAB, None, None),
        P(),
    )
    return jax.shard_map(
        body,
        mesh=finer,
        in_specs=placed,
        out_specs=(P(MODE, None, SLAB, None, None), P(MODE, None), P(MODE, None)),
        check_vma=False,
    )
```

```python
from functools import partial

import jax
import jax.numpy as jnp
from jax import lax
from jax.experimental import pallas as pl
from jax.experimental.pallas import tpu as pltpu
from jax.sharding import Mesh, PartitionSpec as P

CENTER = 110.0
HALF = 90.0
SLAB = ("xh", "z", "y")
MODE = ("xl", "core")
STEPS = (0, 1, -1)
VMEM_LIMIT = 16 * 1024 * 1024


def spec(shape, dtype=jnp.float32):
    return jax.ShapeDtypeStruct(shape, dtype)


def own_index(dz, q, e, dy, c, p):
    return ((((STEPS.index(dz) * 2 + q) * 3 + e) * 3 + STEPS.index(dy)) * 3 + c) * 2 + p


def halo_index(dz, side, e, dy, c):
    return (((STEPS.index(dz) * 2 + side) * 3 + e) * 3 + STEPS.index(dy)) * 3 + c


def rolled(x, by, axis):
    by = by % x.shape[axis]
    return x if by == 0 else pltpu.roll(x, by, axis)


def coefficient_kernel(stiff_ref, layers_ref, own_ref, halo_ref):
    turned = {}
    for layer in range(3):
        for b in range(2):
            for d in range(2):
                turned[layer, b, d] = rolled(rolled(layers_ref[layer], b, 0), d, 1)
    for p in range(2):
        for q in range(-1, 3):
            dx = q - p
            if abs(dx) > 1:
                continue
            for dy in STEPS:
                for dz in STEPS:
                    corners = [
                        (a, b, d)
                        for a in range(2)
                        for b in range(2)
                        for d in range(2)
                        if 0 <= a + dx <= 1 and 0 <= b + dy <= 1 and 0 <= d + dz <= 1
                    ]
                    for c in range(3):
                        for e in range(3):
                            total = None
                            for a, b, d in corners:
                                row = 3 * (4 * a + 2 * b + d) + c
                                col = 3 * (4 * (a + dx) + 2 * (b + dy) + d + dz) + e
                                term = stiff_ref[row, col] * turned[p - a + 1, b + dy, d]
                                total = term if total is None else total + term
                            if 0 <= q <= 1:
                                own_ref[own_index(dz, q, e, dy, c, p)] = total
                            else:
                                halo_ref[halo_index(dz, 0 if q < 0 else 1, e, dy, c)] = total


def coefficients(stiffness, layers):
    rows, depth = layers.shape[1:]
    return pl.pallas_call(
        coefficient_kernel,
        in_specs=[pl.BlockSpec(memory_space=pltpu.SMEM), pl.BlockSpec(memory_space=pltpu.VMEM)],
        out_specs=[pl.BlockSpec(memory_space=pltpu.VMEM)] * 2,
        out_shape=[spec((324, rows, depth)), spec((162, rows, depth))],
        compiler_params=pltpu.CompilerParams(vmem_limit_bytes=VMEM_LIMIT),
    )(stiffness, layers)


OWN_MODES = 2
HALO_MODES = 4
IN_VMEM = pl.BlockSpec(memory_space=pltpu.VMEM)
ANYWHERE = pl.BlockSpec(memory_space=pl.ANY)


def cost(flops, nbytes):
    return pl.CostEstimate(flops=flops, bytes_accessed=nbytes, transcendentals=0)


def compiled():
    return pltpu.CompilerParams(vmem_limit_bytes=VMEM_LIMIT)


def gathered(acc):
    return acc[0] + rolled(acc[1], -1, 0) + rolled(acc[2], 1, 0)


def added(acc, key, term):
    acc[key] = acc[key] + term if key in acc else term


def own_kernel(shift, count, *refs):
    low_ref, high_ref, coef_ref, scale_ref = refs[:4]
    before, parts = refs[4:-2], refs[-2:]
    planes = (low_ref, high_ref)

    def some(i, _):
        base = i * (3 * OWN_MODES)
        acc = {}
        for dz in STEPS:
            for q in range(2):
                for e in range(3):
                    fields = [rolled(planes[q][base + 3 * u + e], -dz, 1) for u in range(OWN_MODES)]
                    for s, dy in enumerate(STEPS):
                        for c in range(3):
                            for p in range(2):
                                coef = coef_ref[own_index(dz, q, e, dy, c, p)]
                                for u in range(OWN_MODES):
                                    added(acc, (u, c, p, s), coef * fields[u])
        for u in range(OWN_MODES):
            for c in range(3):
                at = base + 3 * u + c
                for p in range(2):
                    value = scale_ref[p] * gathered([acc[u, c, p, s] for s in range(3)])
                    if shift:
                        value = value - shift * planes[p][at]
                    if before:
                        value = value - before[p][at]
                    parts[p][at] = value
        return 0

    lax.fori_loop(0, count // (3 * OWN_MODES), some, 0)


def own_part(shift, current, coef, scale, before):
    count, rows, depth = current[0].shape
    args = (*current, coef, scale, *before)
    return pl.pallas_call(
        partial(own_kernel, shift, count),
        in_specs=[IN_VMEM] * len(args),
        out_specs=[IN_VMEM] * 2,
        out_shape=[spec(current[0].shape)] * 2,
        cost_estimate=cost(2 * 108 * count * rows * depth, 16 << 20),
        compiler_params=compiled(),
    )(*args)


def halo_kernel(p, halo_ref, part_ref, coef_ref, scale_ref, out_ref):
    step = 3 * HALO_MODES

    def some(i, _):
        base = i * step
        acc = {}
        for dz in STEPS:
            for e in range(3):
                fields = [rolled(halo_ref[base + 3 * u + e], -dz, 1) for u in range(HALO_MODES)]
                for s, dy in enumerate(STEPS):
                    for c in range(3):
                        coef = coef_ref[halo_index(dz, p, e, dy, c)]
                        for u in range(HALO_MODES):
                            added(acc, (u, c, s), coef * fields[u])
        scale = scale_ref[p]
        for u in range(HALO_MODES):
            for c in range(3):
                at = base + 3 * u + c
                out_ref[at] = part_ref[at] + scale * gathered([acc[u, c, s] for s in range(3)])
        return 0

    lax.fori_loop(0, halo_ref.shape[0] // step, some, 0)


def with_halo(p, halo, part, coef, scale):
    return pl.pallas_call(
        partial(halo_kernel, p),
        in_specs=[IN_VMEM] * 4,
        out_specs=IN_VMEM,
        out_shape=spec(halo.shape),
        cost_estimate=cost(54 * halo.size, 5 << 20),
        compiler_params=compiled(),
    )(halo, part, coef, scale)


def join_kernel(low_ref, high_ref, out_ref):
    def some(i, _):
        out_ref[i, 0] = low_ref[i]
        out_ref[i, 1] = high_ref[i]
        return 0

    lax.fori_loop(0, low_ref.shape[0], some, 0, unroll=8)


def joined(low, high):
    return pl.pallas_call(
        join_kernel,
        in_specs=[IN_VMEM] * 2,
        out_specs=IN_VMEM,
        out_shape=spec((low.shape[0], 2) + low.shape[1:]),
        cost_estimate=cost(1 << 20, 4 << 20),
        compiler_params=compiled(),
    )(low, high)


def split(x):
    top = x.astype(jnp.bfloat16)
    return top, (x - top.astype(jnp.float32)).astype(jnp.bfloat16)


def dot_t(a, b):
    return lax.dot_general(a, b, (((1,), (1,)), ((), ())), preferred_element_type=jnp.float32)


def product(top, rest, left_top, left_rest):
    return dot_t(top, left_top) + dot_t(rest, left_top) + dot_t(top, left_rest)


def each_row(field_ref, modes, do):
    stride, depth = field_ref.shape[0] // modes, field_ref.shape[1]

    def some(row, _):
        do(row, pl.ds(pl.multiple_of(row * depth, depth), depth))
        return 0

    lax.fori_loop(0, stride, some, 0, unroll=4)


def modes_at(ref, row, modes):
    return ref[pl.ds(row, modes, stride=ref.shape[0] // modes), :]


def held(x, *after):
    return pl.pallas_call(
        lambda *refs: None,
        in_specs=[ANYWHERE] * (1 + len(after)),
        out_specs=ANYWHERE,
        out_shape=spec(x.shape),
        input_output_aliases={0: 0},
        cost_estimate=cost(0, 1 << 10),
        compiler_params=compiled(),
    )(x, *after)


def near_kernel(stiff_ref, own_ref, field_ref, mass_ref, left_top, left_rest, out_ref, top, rest):
    modes = top.shape[0] // 2
    first, second = pl.ds(0, modes), pl.ds(modes, modes)

    def do(row, at):
        own = modes_at(own_ref, row, modes)
        weight = mass_ref[pl.ds(lax.rem(row, mass_ref.shape[0]), 1), :]
        left_top[first, at], left_rest[first, at] = split(modes_at(stiff_ref, row, modes))
        left_top[second, at], left_rest[second, at] = split(own * weight)
        top[first, at], rest[first, at] = split(own)
        top[second, at], rest[second, at] = split(modes_at(field_ref, row, modes))

    each_row(own_ref, modes, do)
    out_ref[...] = product(top[...], rest[...], left_top[...], left_rest[...])


def near_gram(stiff, own, by_x, mass, modes):
    wide = own.size // modes
    shape = (2 * modes, wide)
    depth = mass.shape[-1]
    return pl.pallas_call(
        near_kernel,
        in_specs=[IN_VMEM] * 4,
        out_specs=[IN_VMEM] * 3,
        out_shape=[spec(shape, jnp.bfloat16)] * 2 + [spec((2 * modes, 2 * modes))],
        scratch_shapes=[pltpu.VMEM(shape, jnp.bfloat16)] * 2,
        cost_estimate=cost(1 << 20, 8 << 20),
        compiler_params=compiled(),
    )(*(a.reshape(-1, depth) for a in (stiff, own, by_x)), mass)


def far_product(core_ref, both_ref, left_top, left_rest, top, rest):
    modes = top.shape[0] // 2
    first, second = pl.ds(0, modes), pl.ds(modes, modes)

    def do(row, at):
        top[first, at], rest[first, at] = split(modes_at(core_ref, row, modes))
        top[second, at], rest[second, at] = split(modes_at(both_ref, row, modes))

    each_row(core_ref, modes, do)
    return product(top[...], rest[...], left_top[...], left_rest[...])


def far_kernel(core_ref, both_ref, left_top, left_rest, out_ref, top, rest):
    out_ref[...] = far_product(core_ref, both_ref, left_top, left_rest, top, rest)


def last_kernel(factor, core_ref, both_ref, left_top, left_rest, place_ref, *refs):
    nears, fars, out_ref, top, rest, turned = refs[:2], refs[2:-4], *refs[-4:]
    far = far_product(core_ref, both_ref, left_top, left_rest, top, rest)
    modes = top.shape[0] // 2
    far = far + fars[0][...]
    near = nears[0][...] + nears[1][...]
    blocks = (near[:modes], far[:modes], near[modes:], far[modes:])
    for r in range(4):
        at = pl.ds(pl.multiple_of(place_ref[r] * modes, modes), modes)
        turned[at, :] = blocks[r] * factor
    whole = turned[...].T
    out_ref[0 : 2 * modes, :] = whole[:, :128]
    tail = whole[:, 128:]
    out_ref[2 * modes :, :] = jnp.concatenate([tail[:modes], tail[modes:]], 1)


def far_gram(by_core, by_both, left, modes, last=None):
    wide = by_core.size // modes
    shape = (2 * modes, wide)
    depth = by_core.shape[-1]
    args = [a.reshape(-1, depth) for a in (by_core, by_both)] + list(left)
    specs = [IN_VMEM] * 4
    scratch = [pltpu.VMEM(shape, jnp.bfloat16)] * 2
    if last is None:
        kernel, out = far_kernel, (2 * modes, 2 * modes)
    else:
        factor, place, nears, fars = last
        kernel, out = partial(last_kernel, factor), (3 * modes, 128)
        args += [place, *nears, *fars]
        specs += [pl.BlockSpec(memory_space=pltpu.SMEM)] + [IN_VMEM] * 3
        scratch.append(pltpu.VMEM((4 * modes, 2 * modes), jnp.float32))
    return pl.pallas_call(
        kernel,
        in_specs=specs,
        out_specs=IN_VMEM,
        out_shape=spec(out),
        scratch_shapes=scratch,
        cost_estimate=cost(1 << 20, 8 << 20),
        compiler_params=compiled(),
    )(*args)


def total_over(x, axes, groups):
    above, count, below = groups
    parts = []
    for k in range(1, count):
        pairs = [
            ((i * count + j) * below + l, (i * count + (j + k) % count) * below + l)
            for i in range(above)
            for j in range(count)
            for l in range(below)
        ]
        parts.append(lax.ppermute(x, axes, pairs))
    for part in parts:
        x = x + part
    return x


def body(subspace, modulus, mass, support, stiffness):
    modes, comps, planes, rows, depth = subspace.shape
    slabs = lax.axis_size(SLAB)
    four = lax.axis_size(MODE)
    up = [
        (i * four + m, (i + 1) * four + m if i + 1 < slabs else m ^ 2)
        for i in range(slabs)
        for m in range(four)
    ]
    down = [(b, a) for a, b in up]
    everywhere = SLAB + MODE
    lower_layer = lax.ppermute(modulus[planes - 1 :], everywhere, up)
    free = (1 - support).astype(jnp.float32)

    def masked(p):
        return (free[p] * subspace[:, :, p]).reshape(modes * comps, rows, depth)

    current = (masked(0), masked(1))
    layers = jnp.concatenate([lower_layer, modulus], 0)
    plane_index = (
        lax.axis_index(SLAB) * planes - 1 + lax.broadcasted_iota(jnp.int32, layers.shape, 0)
    )
    row_index = lax.broadcasted_iota(jnp.int32, layers.shape, 1)
    depth_index = lax.broadcasted_iota(jnp.int32, layers.shape, 2)
    valid = (
        (plane_index >= 0)
        & (plane_index < planes * slabs - 1)
        & (row_index < rows - 1)
        & (depth_index < depth - 1)
    )
    layers = jnp.where(valid, layers, jnp.zeros_like(layers))
    own_coef, halo_coef = coefficients(stiffness, layers)
    scale = free / (mass * HALF)

    before = ()
    lower = lax.ppermute(current[1], everywhere, up)
    upper = lax.ppermute(current[0], everywhere, down)
    for k in range(4):
        times = 1.0 if k == 0 else 2.0
        part = own_part(times * CENTER / HALF, current, own_coef, times * scale, before)
        high = with_halo(1, upper, part[1], halo_coef, times * scale)
        below = lax.ppermute(high, everywhere, up)
        low = with_halo(0, lower, part[0], halo_coef, times * scale)
        upper = lax.ppermute(low, everywhere, down)
        lower = below
        before, current = current, (low, high)
    swap = [(0, 1), (1, 0)]
    by_x = [None, None]
    for p in (1, 0):
        by_x[p] = lax.ppermute(current[p], "xl", swap)
    filtered = joined(*current)
    part = own_part(0.0, current, own_coef, free, ())
    stiffened = [with_halo(p, h, part[p], halo_coef, free) for p, h in ((0, lower), (1, upper))]
    me = lax.axis_index(MODE)
    place = jnp.stack([me ^ r for r in range(4)]).astype(jnp.int32)
    factor = 1.0 / (float(comps) * planes * slabs * rows * depth)
    nears, fars = [], []
    after = (*stiffened, filtered)
    for p in (1, 0):
        by_x[p] = held(by_x[p], *after)
        by_core = lax.ppermute(current[p], "core", swap)
        by_both = lax.ppermute(by_x[p], "core", swap)
        *left, near = near_gram(stiffened[p], current[p], by_x[p], mass[p], modes)
        nears.append(near)
        after = (near,)
        last = (factor, place, nears, fars) if p == 0 else None
        fars.append(far_gram(by_core, by_both, left, modes, last))
    grams = fars[-1]
    for groups in ((16, 4, 1), (4, 4, 4), (2, 2, 16), (1, 2, 32)):
        grams = total_over(grams, SLAB, groups)
    tail = grams[2 * modes :]
    wide = 4 * modes - depth
    stiffness_gram = jnp.concatenate([grams[:modes], tail[:, :wide]], 1)
    mass_gram = jnp.concatenate([grams[modes : 2 * modes], tail[:, wide:]], 1)
    return filtered.reshape(subspace.shape), stiffness_gram, mass_gram


def solution(mesh):
    finer = Mesh(mesh.devices.reshape(2, 8, 4, 2, 2), SLAB + MODE)
    placed = (
        P(MODE, None, SLAB, None, None),
        P(SLAB, None, None),
        P(SLAB, None, None),
        P(SLAB, None, None),
        P(),
    )
    return jax.shard_map(
        body,
        mesh=finer,
        in_specs=placed,
        out_specs=(P(MODE, None, SLAB, None, None), P(MODE, None), P(MODE, None)),
        check_vma=False,
    )
```

```python
from functools import partial

import jax
import jax.numpy as jnp
from jax import lax
from jax.experimental import pallas as pl
from jax.experimental.pallas import tpu as pltpu
from jax.sharding import Mesh, PartitionSpec as P

CENTER = 110.0
HALF = 90.0
SLAB = ("xh", "z", "y")
MODE = ("xl", "core")
STEPS = (0, 1, -1)
VMEM_LIMIT = 16 * 1024 * 1024


def spec(shape, dtype=jnp.float32):
    return jax.ShapeDtypeStruct(shape, dtype)


def own_index(dz, q, e, dy, c, p):
    return ((((STEPS.index(dz) * 2 + q) * 3 + e) * 3 + STEPS.index(dy)) * 3 + c) * 2 + p


def halo_index(dz, side, e, dy, c):
    return (((STEPS.index(dz) * 2 + side) * 3 + e) * 3 + STEPS.index(dy)) * 3 + c


def rolled(x, by, axis):
    by = by % x.shape[axis]
    return x if by == 0 else pltpu.roll(x, by, axis)


def coefficient_kernel(stiff_ref, layers_ref, own_ref, halo_ref):
    turned = {}
    for layer in range(3):
        for b in range(2):
            for d in range(2):
                turned[layer, b, d] = rolled(rolled(layers_ref[layer], b, 0), d, 1)
    for p in range(2):
        for q in range(-1, 3):
            dx = q - p
            if abs(dx) > 1:
                continue
            for dy in STEPS:
                for dz in STEPS:
                    corners = [
                        (a, b, d)
                        for a in range(2)
                        for b in range(2)
                        for d in range(2)
                        if 0 <= a + dx <= 1 and 0 <= b + dy <= 1 and 0 <= d + dz <= 1
                    ]
                    for c in range(3):
                        for e in range(3):
                            total = None
                            for a, b, d in corners:
                                row = 3 * (4 * a + 2 * b + d) + c
                                col = 3 * (4 * (a + dx) + 2 * (b + dy) + d + dz) + e
                                term = stiff_ref[row, col] * turned[p - a + 1, b + dy, d]
                                total = term if total is None else total + term
                            if 0 <= q <= 1:
                                own_ref[own_index(dz, q, e, dy, c, p)] = total
                            else:
                                halo_ref[halo_index(dz, 0 if q < 0 else 1, e, dy, c)] = total


def coefficients(stiffness, layers):
    rows, depth = layers.shape[1:]
    return pl.pallas_call(
        coefficient_kernel,
        in_specs=[pl.BlockSpec(memory_space=pltpu.SMEM), pl.BlockSpec(memory_space=pltpu.VMEM)],
        out_specs=[pl.BlockSpec(memory_space=pltpu.VMEM)] * 2,
        out_shape=[spec((324, rows, depth)), spec((162, rows, depth))],
        compiler_params=pltpu.CompilerParams(vmem_limit_bytes=VMEM_LIMIT),
    )(stiffness, layers)


OWN_MODES = 2
HALO_MODES = 4
IN_VMEM = pl.BlockSpec(memory_space=pltpu.VMEM)
ANYWHERE = pl.BlockSpec(memory_space=pl.ANY)


def cost(flops, nbytes):
    return pl.CostEstimate(flops=flops, bytes_accessed=nbytes, transcendentals=0)


def compiled():
    return pltpu.CompilerParams(vmem_limit_bytes=VMEM_LIMIT)


def gathered(acc):
    return acc[0] + rolled(acc[1], -1, 0) + rolled(acc[2], 1, 0)


def start_kernel(field_ref, support_ref, modulus_ref, low_ref, high_ref, edge_ref):
    free = [(1 - support_ref[p]).astype(jnp.float32) for p in range(2)]
    low_ref[...] = field_ref[:, 0] * free[0]
    high_ref[...] = field_ref[:, 1] * free[1]
    edge_ref[0] = modulus_ref[1]


def start(field, support, modulus):
    count, planes, rows, depth = field.shape
    tile = count // 4
    plane = pl.BlockSpec((tile, rows, depth), lambda i: (i, 0, 0))
    edge = pl.BlockSpec((1, rows, depth), lambda i: (0, 0, 0))
    both = pl.BlockSpec((planes, rows, depth), lambda i: (0, 0, 0))
    return pl.pallas_call(
        start_kernel,
        grid=(4,),
        in_specs=[pl.BlockSpec((tile, planes, rows, depth), lambda i: (i, 0, 0, 0)), both, both],
        out_specs=[plane, plane, edge],
        out_shape=[spec((count, rows, depth))] * 2 + [spec((1, rows, depth))],
        cost_estimate=cost(2 * field.size, 8 * field.size),
        compiler_params=compiled(),
    )(field, support, modulus)


def added(acc, key, term):
    acc[key] = acc[key] + term if key in acc else term


def own_kernel(shift, count, *refs):
    low_ref, high_ref, coef_ref, scale_ref = refs[:4]
    before, parts = refs[4:-2], refs[-2:]
    planes = (low_ref, high_ref)

    def some(i, _):
        base = i * (3 * OWN_MODES)
        acc = {}
        for dz in STEPS:
            for q in range(2):
                for e in range(3):
                    fields = [rolled(planes[q][base + 3 * u + e], -dz, 1) for u in range(OWN_MODES)]
                    for s, dy in enumerate(STEPS):
                        for c in range(3):
                            for p in range(2):
                                coef = coef_ref[own_index(dz, q, e, dy, c, p)]
                                for u in range(OWN_MODES):
                                    added(acc, (u, c, p, s), coef * fields[u])
        for u in range(OWN_MODES):
            for c in range(3):
                at = base + 3 * u + c
                for p in range(2):
                    value = scale_ref[p] * gathered([acc[u, c, p, s] for s in range(3)])
                    if shift:
                        value = value - shift * planes[p][at]
                    if before:
                        value = value - before[p][at]
                    parts[p][at] = value
        return 0

    lax.fori_loop(0, count // (3 * OWN_MODES), some, 0)


def own_part(shift, current, coef, scale, before):
    count, rows, depth = current[0].shape
    args = (*current, coef, scale, *before)
    return pl.pallas_call(
        partial(own_kernel, shift, count),
        in_specs=[IN_VMEM] * len(args),
        out_specs=[IN_VMEM] * 2,
        out_shape=[spec(current[0].shape)] * 2,
        cost_estimate=cost(2 * 108 * count * rows * depth, 16 << 20),
        compiler_params=compiled(),
    )(*args)


def halo_kernel(p, halo_ref, part_ref, coef_ref, scale_ref, out_ref):
    step = 3 * HALO_MODES

    def some(i, _):
        base = i * step
        acc = {}
        for dz in STEPS:
            for e in range(3):
                fields = [rolled(halo_ref[base + 3 * u + e], -dz, 1) for u in range(HALO_MODES)]
                for s, dy in enumerate(STEPS):
                    for c in range(3):
                        coef = coef_ref[halo_index(dz, p, e, dy, c)]
                        for u in range(HALO_MODES):
                            added(acc, (u, c, s), coef * fields[u])
        scale = scale_ref[p]
        for u in range(HALO_MODES):
            for c in range(3):
                at = base + 3 * u + c
                out_ref[at] = part_ref[at] + scale * gathered([acc[u, c, s] for s in range(3)])
        return 0

    lax.fori_loop(0, halo_ref.shape[0] // step, some, 0)


def with_halo(p, halo, part, coef, scale):
    return pl.pallas_call(
        partial(halo_kernel, p),
        in_specs=[IN_VMEM] * 4,
        out_specs=IN_VMEM,
        out_shape=spec(halo.shape),
        cost_estimate=cost(54 * halo.size, 5 << 20),
        compiler_params=compiled(),
    )(halo, part, coef, scale)


def join_kernel(low_ref, high_ref, out_ref):
    def some(i, _):
        out_ref[i, 0] = low_ref[i]
        out_ref[i, 1] = high_ref[i]
        return 0

    lax.fori_loop(0, low_ref.shape[0], some, 0, unroll=8)


def joined(low, high):
    return pl.pallas_call(
        join_kernel,
        in_specs=[IN_VMEM] * 2,
        out_specs=IN_VMEM,
        out_shape=spec((low.shape[0], 2) + low.shape[1:]),
        cost_estimate=cost(1 << 20, 4 << 20),
        compiler_params=compiled(),
    )(low, high)


def split(x):
    top = x.astype(jnp.bfloat16)
    return top, (x - top.astype(jnp.float32)).astype(jnp.bfloat16)


def dot_t(a, b):
    return lax.dot_general(a, b, (((1,), (1,)), ((), ())), preferred_element_type=jnp.float32)


def product(top, rest, left_top, left_rest):
    return dot_t(top, left_top) + dot_t(rest, left_top) + dot_t(top, left_rest)


def each_row(field_ref, modes, do):
    stride, depth = field_ref.shape[0] // modes, field_ref.shape[1]

    def some(row, _):
        do(row, pl.ds(pl.multiple_of(row * depth, depth), depth))
        return 0

    lax.fori_loop(0, stride, some, 0, unroll=4)


def modes_at(ref, row, modes):
    return ref[pl.ds(row, modes, stride=ref.shape[0] // modes), :]


def held(x, *after):
    return pl.pallas_call(
        lambda *refs: None,
        in_specs=[ANYWHERE] * (1 + len(after)),
        out_specs=ANYWHERE,
        out_shape=spec(x.shape),
        input_output_aliases={0: 0},
        cost_estimate=cost(0, 1 << 10),
        compiler_params=compiled(),
    )(x, *after)


def near_kernel(stiff_ref, own_ref, field_ref, mass_ref, *refs):
    left_top, left_rest, out_ref, top, rest = refs[-5:]
    modes = top.shape[0] // 2
    first, second = pl.ds(0, modes), pl.ds(modes, modes)

    def do(row, at):
        own = modes_at(own_ref, row, modes)
        weight = mass_ref[pl.ds(lax.rem(row, mass_ref.shape[0]), 1), :]
        left_top[first, at], left_rest[first, at] = split(modes_at(stiff_ref, row, modes))
        left_top[second, at], left_rest[second, at] = split(own * weight)
        top[first, at], rest[first, at] = split(own)
        top[second, at], rest[second, at] = split(modes_at(field_ref, row, modes))

    each_row(own_ref, modes, do)
    out_ref[...] = product(top[...], rest[...], left_top[...], left_rest[...])


def near_gram(stiff, own, by_x, mass, modes, after=()):
    wide = own.size // modes
    shape = (2 * modes, wide)
    depth = mass.shape[-1]
    return pl.pallas_call(
        near_kernel,
        in_specs=[IN_VMEM] * 4 + [ANYWHERE] * len(after),
        out_specs=[IN_VMEM] * 3,
        out_shape=[spec(shape, jnp.bfloat16)] * 2 + [spec((2 * modes, 2 * modes))],
        scratch_shapes=[pltpu.VMEM(shape, jnp.bfloat16)] * 2,
        cost_estimate=cost(1 << 20, 8 << 20),
        compiler_params=compiled(),
    )(*(a.reshape(-1, depth) for a in (stiff, own, by_x)), mass, *after)


def far_product(p, core_ref, both_ref, left_top, left_rest, top, rest):
    modes = top.shape[0] // 2
    first, second = pl.ds(0, modes), pl.ds(modes, modes)
    rows = top.shape[1] // (3 * both_ref.shape[1])

    def do(row, at):
        comp, inner = lax.div(row, rows), lax.rem(row, rows)
        core_row = (2 * comp + p) * rows + inner
        top[first, at], rest[first, at] = split(modes_at(core_ref, core_row, modes))
        top[second, at], rest[second, at] = split(modes_at(both_ref, row, modes))

    each_row(both_ref, modes, do)
    return product(top[...], rest[...], left_top[...], left_rest[...])


def far_kernel(p, core_ref, both_ref, left_top, left_rest, out_ref, top, rest):
    out_ref[...] = far_product(p, core_ref, both_ref, left_top, left_rest, top, rest)


def last_kernel(factor, p, core_ref, both_ref, left_top, left_rest, place_ref, *refs):
    nears, fars, out_ref, top, rest, turned = refs[:2], refs[2:-4], *refs[-4:]
    far = far_product(p, core_ref, both_ref, left_top, left_rest, top, rest)
    modes = top.shape[0] // 2
    far = far + fars[0][...]
    near = nears[0][...] + nears[1][...]
    blocks = (near[:modes], far[:modes], near[modes:], far[modes:])
    for r in range(4):
        at = pl.ds(pl.multiple_of(place_ref[r] * modes, modes), modes)
        turned[at, :] = blocks[r] * factor
    whole = turned[...].T
    out_ref[0 : 2 * modes, :] = whole[:, :128]
    tail = whole[:, 128:]
    out_ref[2 * modes :, :] = jnp.concatenate([tail[:modes], tail[modes:]], 1)


def far_gram(p, by_core, by_both, left, modes, last=None):
    wide = by_both.size // modes
    shape = (2 * modes, wide)
    depth = by_core.shape[-1]
    args = [a.reshape(-1, depth) for a in (by_core, by_both)] + list(left)
    specs = [IN_VMEM] * 4
    scratch = [pltpu.VMEM(shape, jnp.bfloat16)] * 2
    if last is None:
        kernel, out = partial(far_kernel, p), (2 * modes, 2 * modes)
    else:
        factor, place, nears, fars = last
        kernel, out = partial(last_kernel, factor, p), (3 * modes, 128)
        args += [place, *nears, *fars]
        specs += [pl.BlockSpec(memory_space=pltpu.SMEM)] + [IN_VMEM] * 3
        scratch.append(pltpu.VMEM((4 * modes, 2 * modes), jnp.float32))
    return pl.pallas_call(
        kernel,
        in_specs=specs,
        out_specs=IN_VMEM,
        out_shape=spec(out),
        scratch_shapes=scratch,
        cost_estimate=cost(1 << 20, 8 << 20),
        compiler_params=compiled(),
    )(*args)


def total_over(x, axes, groups):
    above, count, below = groups
    parts = []
    for k in range(1, count):
        pairs = [
            ((i * count + j) * below + l, (i * count + (j + k) % count) * below + l)
            for i in range(above)
            for j in range(count)
            for l in range(below)
        ]
        parts.append(lax.ppermute(x, axes, pairs))
    for part in parts:
        x = x + part
    return x


def body(subspace, modulus, mass, support, stiffness):
    modes, comps, planes, rows, depth = subspace.shape
    slabs = lax.axis_size(SLAB)
    four = lax.axis_size(MODE)
    up = [
        (i * four + m, (i + 1) * four + m if i + 1 < slabs else m ^ 2)
        for i in range(slabs)
        for m in range(four)
    ]
    down = [(b, a) for a, b in up]
    everywhere = SLAB + MODE
    *current, edge = start(
        subspace.reshape(modes * comps, planes, rows, depth), support, modulus
    )
    lower_layer = lax.ppermute(edge, everywhere, up)
    free = (1 - support).astype(jnp.float32)
    layers = jnp.concatenate([lower_layer, modulus], 0)
    plane_index = (
        lax.axis_index(SLAB) * planes - 1 + lax.broadcasted_iota(jnp.int32, layers.shape, 0)
    )
    row_index = lax.broadcasted_iota(jnp.int32, layers.shape, 1)
    depth_index = lax.broadcasted_iota(jnp.int32, layers.shape, 2)
    valid = (
        (plane_index >= 0)
        & (plane_index < planes * slabs - 1)
        & (row_index < rows - 1)
        & (depth_index < depth - 1)
    )
    layers = jnp.where(valid, layers, jnp.zeros_like(layers))
    own_coef, halo_coef = coefficients(stiffness, layers)
    scale = free / (mass * HALF)

    before = ()
    lower = lax.ppermute(current[1], everywhere, up)
    upper = lax.ppermute(current[0], everywhere, down)
    for k in range(4):
        times = 1.0 if k == 0 else 2.0
        part = own_part(times * CENTER / HALF, current, own_coef, times * scale, before)
        high = with_halo(1, upper, part[1], halo_coef, times * scale)
        below = lax.ppermute(high, everywhere, up)
        low = with_halo(0, lower, part[0], halo_coef, times * scale)
        upper = lax.ppermute(low, everywhere, down)
        lower = below
        before, current = current, (low, high)
    swap = [(0, 1), (1, 0)]
    by_x = [None, None]
    for p in (1, 0):
        by_x[p] = lax.ppermute(current[p], "xl", swap)
    filtered = joined(*current)
    part = own_part(0.0, current, own_coef, free, ())
    stiffened = [with_halo(p, h, part[p], halo_coef, free) for p, h in ((0, lower), (1, upper))]
    me = lax.axis_index(MODE)
    place = jnp.stack([me ^ r for r in range(4)]).astype(jnp.int32)
    factor = 1.0 / (float(comps) * planes * slabs * rows * depth)
    by_core = lax.ppermute(filtered, "core", swap)
    nears, fars = [], []
    after = (*stiffened, filtered)
    for p in (1, 0):
        by_x[p] = held(by_x[p], *after)
        by_both = lax.ppermute(by_x[p], "core", swap)
        *left, near = near_gram(
            stiffened[p], current[p], by_x[p], mass[p], modes, by_x[:1] if p else ()
        )
        nears.append(near)
        last = (factor, place, nears, fars) if p == 0 else None
        fars.append(far_gram(p, by_core, by_both, left, modes, last))
        after = (near, fars[0])
    grams = fars[-1]
    for groups in ((16, 4, 1), (8, 2, 4), (2, 4, 8), (1, 2, 32)):
        grams = total_over(grams, SLAB, groups)
    tail = grams[2 * modes :]
    wide = 4 * modes - depth
    stiffness_gram = jnp.concatenate([grams[:modes], tail[:, :wide]], 1)
    mass_gram = jnp.concatenate([grams[modes : 2 * modes], tail[:, wide:]], 1)
    return filtered.reshape(subspace.shape), stiffness_gram, mass_gram


def solution(mesh):
    finer = Mesh(mesh.devices.reshape(2, 8, 4, 2, 2), SLAB + MODE)
    placed = (
        P(MODE, None, SLAB, None, None),
        P(SLAB, None, None),
        P(SLAB, None, None),
        P(SLAB, None, None),
        P(),
    )
    return jax.shard_map(
        body,
        mesh=finer,
        in_specs=placed,
        out_specs=(P(MODE, None, SLAB, None, None), P(MODE, None), P(MODE, None)),
        check_vma=False,
    )
```

```python
from functools import partial

import jax
import jax.numpy as jnp
from jax import lax
from jax.experimental import pallas as pl
from jax.experimental.pallas import tpu as pltpu
from jax.sharding import Mesh, PartitionSpec as P

CENTER = 110.0
HALF = 90.0
SLAB = ("xh", "z", "y")
MODE = ("xl", "core")
STEPS = (0, 1, -1)
VMEM_LIMIT = 16 * 1024 * 1024


def spec(shape, dtype=jnp.float32):
    return jax.ShapeDtypeStruct(shape, dtype)


def own_index(dz, q, e, dy, c, p):
    return ((((STEPS.index(dz) * 2 + q) * 3 + e) * 3 + STEPS.index(dy)) * 3 + c) * 2 + p


def halo_index(dz, side, e, dy, c):
    return (((STEPS.index(dz) * 2 + side) * 3 + e) * 3 + STEPS.index(dy)) * 3 + c


def rolled(x, by, axis):
    by = by % x.shape[axis]
    return x if by == 0 else pltpu.roll(x, by, axis)


def coefficient_kernel(stiff_ref, layers_ref, own_ref, halo_ref):
    turned = {}
    for layer in range(3):
        for b in range(2):
            for d in range(2):
                turned[layer, b, d] = rolled(rolled(layers_ref[layer], b, 0), d, 1)
    for p in range(2):
        for q in range(-1, 3):
            dx = q - p
            if abs(dx) > 1:
                continue
            for dy in STEPS:
                for dz in STEPS:
                    corners = [
                        (a, b, d)
                        for a in range(2)
                        for b in range(2)
                        for d in range(2)
                        if 0 <= a + dx <= 1 and 0 <= b + dy <= 1 and 0 <= d + dz <= 1
                    ]
                    for c in range(3):
                        for e in range(3):
                            total = None
                            for a, b, d in corners:
                                row = 3 * (4 * a + 2 * b + d) + c
                                col = 3 * (4 * (a + dx) + 2 * (b + dy) + d + dz) + e
                                term = stiff_ref[row, col] * turned[p - a + 1, b + dy, d]
                                total = term if total is None else total + term
                            if 0 <= q <= 1:
                                own_ref[own_index(dz, q, e, dy, c, p)] = total
                            else:
                                halo_ref[halo_index(dz, 0 if q < 0 else 1, e, dy, c)] = total


def coefficients(stiffness, layers):
    rows, depth = layers.shape[1:]
    return pl.pallas_call(
        coefficient_kernel,
        in_specs=[pl.BlockSpec(memory_space=pltpu.SMEM), pl.BlockSpec(memory_space=pltpu.VMEM)],
        out_specs=[pl.BlockSpec(memory_space=pltpu.VMEM)] * 2,
        out_shape=[spec((324, rows, depth)), spec((162, rows, depth))],
        compiler_params=pltpu.CompilerParams(vmem_limit_bytes=VMEM_LIMIT),
    )(stiffness, layers)


OWN_MODES = 2
HALO_MODES = 4
IN_VMEM = pl.BlockSpec(memory_space=pltpu.VMEM)
ANYWHERE = pl.BlockSpec(memory_space=pl.ANY)


def cost(flops, nbytes):
    return pl.CostEstimate(flops=flops, bytes_accessed=nbytes, transcendentals=0)


def compiled():
    return pltpu.CompilerParams(vmem_limit_bytes=VMEM_LIMIT)


def gathered(acc):
    return acc[0] + rolled(acc[1], -1, 0) + rolled(acc[2], 1, 0)


def start_kernel(field_ref, support_ref, modulus_ref, low_ref, high_ref, edge_ref, field, support, sems):
    parts = sems.shape[0] - 2
    tile = field.shape[0] // parts
    copies = [
        pltpu.make_async_copy(support_ref, support, sems.at[parts]),
        pltpu.make_async_copy(modulus_ref.at[pl.ds(1, 1)], edge_ref, sems.at[parts + 1]),
    ]
    for i in range(parts):
        rows = pl.ds(i * tile, tile)
        copies.append(pltpu.make_async_copy(field_ref.at[rows], field.at[rows], sems.at[i]))
    for copy in copies:
        copy.start()
    copies[0].wait()
    free = [(1 - support[p]).astype(jnp.float32) for p in range(2)]
    for i in range(parts):
        copies[2 + i].wait()
        rows = pl.ds(i * tile, tile)
        low_ref[rows] = field[rows, 0] * free[0]
        high_ref[rows] = field[rows, 1] * free[1]
    copies[1].wait()


def start(field, support, modulus):
    count, planes, rows, depth = field.shape
    parts = 4
    return pl.pallas_call(
        start_kernel,
        in_specs=[ANYWHERE] * 3,
        out_specs=[IN_VMEM] * 3,
        out_shape=[spec((count, rows, depth))] * 2 + [spec((1, rows, depth))],
        scratch_shapes=[
            pltpu.VMEM(field.shape, jnp.float32),
            pltpu.VMEM(support.shape, support.dtype),
            pltpu.SemaphoreType.DMA((parts + 2,)),
        ],
        cost_estimate=cost(2 * field.size, 8 * field.size),
        compiler_params=pltpu.CompilerParams(vmem_limit_bytes=60 * 1024 * 1024),
    )(field, support, modulus)


def added(acc, key, term):
    acc[key] = acc[key] + term if key in acc else term


def own_kernel(shift, count, *refs):
    low_ref, high_ref, coef_ref, scale_ref = refs[:4]
    before, parts = refs[4:-2], refs[-2:]
    planes = (low_ref, high_ref)

    def some(i, _):
        base = i * (3 * OWN_MODES)
        acc = {}
        for dz in STEPS:
            for q in range(2):
                for e in range(3):
                    fields = [rolled(planes[q][base + 3 * u + e], -dz, 1) for u in range(OWN_MODES)]
                    for s, dy in enumerate(STEPS):
                        for c in range(3):
                            for p in range(2):
                                coef = coef_ref[own_index(dz, q, e, dy, c, p)]
                                for u in range(OWN_MODES):
                                    added(acc, (u, c, p, s), coef * fields[u])
        for u in range(OWN_MODES):
            for c in range(3):
                at = base + 3 * u + c
                for p in range(2):
                    value = scale_ref[p] * gathered([acc[u, c, p, s] for s in range(3)])
                    if shift:
                        value = value - shift * planes[p][at]
                    if before:
                        value = value - before[p][at]
                    parts[p][at] = value
        return 0

    lax.fori_loop(0, count // (3 * OWN_MODES), some, 0)


def own_part(shift, current, coef, scale, before):
    count, rows, depth = current[0].shape
    args = (*current, coef, scale, *before)
    return pl.pallas_call(
        partial(own_kernel, shift, count),
        in_specs=[IN_VMEM] * len(args),
        out_specs=[IN_VMEM] * 2,
        out_shape=[spec(current[0].shape)] * 2,
        cost_estimate=cost(2 * 108 * count * rows * depth, 16 << 20),
        compiler_params=compiled(),
    )(*args)


def halo_kernel(p, halo_ref, part_ref, coef_ref, scale_ref, out_ref):
    step = 3 * HALO_MODES

    def some(i, _):
        base = i * step
        acc = {}
        for dz in STEPS:
            for e in range(3):
                fields = [rolled(halo_ref[base + 3 * u + e], -dz, 1) for u in range(HALO_MODES)]
                for s, dy in enumerate(STEPS):
                    for c in range(3):
                        coef = coef_ref[halo_index(dz, p, e, dy, c)]
                        for u in range(HALO_MODES):
                            added(acc, (u, c, s), coef * fields[u])
        scale = scale_ref[p]
        for u in range(HALO_MODES):
            for c in range(3):
                at = base + 3 * u + c
                out_ref[at] = part_ref[at] + scale * gathered([acc[u, c, s] for s in range(3)])
        return 0

    lax.fori_loop(0, halo_ref.shape[0] // step, some, 0)


def with_halo(p, halo, part, coef, scale):
    return pl.pallas_call(
        partial(halo_kernel, p),
        in_specs=[IN_VMEM] * 4,
        out_specs=IN_VMEM,
        out_shape=spec(halo.shape),
        cost_estimate=cost(54 * halo.size, 5 << 20),
        compiler_params=compiled(),
    )(halo, part, coef, scale)


def join_kernel(low_ref, high_ref, out_ref):
    def some(i, _):
        out_ref[i, 0] = low_ref[i]
        out_ref[i, 1] = high_ref[i]
        return 0

    lax.fori_loop(0, low_ref.shape[0], some, 0, unroll=8)


def joined(low, high):
    return pl.pallas_call(
        join_kernel,
        in_specs=[IN_VMEM] * 2,
        out_specs=IN_VMEM,
        out_shape=spec((low.shape[0], 2) + low.shape[1:]),
        cost_estimate=cost(1 << 20, 4 << 20),
        compiler_params=compiled(),
    )(low, high)


def split(x):
    top = x.astype(jnp.bfloat16)
    return top, (x - top.astype(jnp.float32)).astype(jnp.bfloat16)


def dot_t(a, b):
    return lax.dot_general(a, b, (((1,), (1,)), ((), ())), preferred_element_type=jnp.float32)


def product(top, rest, left_top, left_rest):
    return dot_t(top, left_top) + dot_t(rest, left_top) + dot_t(top, left_rest)


def each_row(field_ref, modes, do):
    stride, depth = field_ref.shape[0] // modes, field_ref.shape[1]

    def some(row, _):
        do(row, pl.ds(pl.multiple_of(row * depth, depth), depth))
        return 0

    lax.fori_loop(0, stride, some, 0, unroll=4)


def modes_at(ref, row, modes):
    return ref[pl.ds(row, modes, stride=ref.shape[0] // modes), :]


def held(x, *after):
    return pl.pallas_call(
        lambda *refs: None,
        in_specs=[ANYWHERE] * (1 + len(after)),
        out_specs=ANYWHERE,
        out_shape=spec(x.shape),
        input_output_aliases={0: 0},
        cost_estimate=cost(0, 1 << 10),
        compiler_params=compiled(),
    )(x, *after)


def near_kernel(stiff_ref, own_ref, field_ref, mass_ref, *refs):
    left_top, left_rest, out_ref, top, rest = refs[-5:]
    modes = top.shape[0] // 2
    first, second = pl.ds(0, modes), pl.ds(modes, modes)

    def do(row, at):
        own = modes_at(own_ref, row, modes)
        weight = mass_ref[pl.ds(lax.rem(row, mass_ref.shape[0]), 1), :]
        left_top[first, at], left_rest[first, at] = split(modes_at(stiff_ref, row, modes))
        left_top[second, at], left_rest[second, at] = split(own * weight)
        top[first, at], rest[first, at] = split(own)
        top[second, at], rest[second, at] = split(modes_at(field_ref, row, modes))

    each_row(own_ref, modes, do)
    out_ref[...] = product(top[...], rest[...], left_top[...], left_rest[...])


def near_gram(stiff, own, by_x, mass, modes, after=()):
    wide = own.size // modes
    shape = (2 * modes, wide)
    depth = mass.shape[-1]
    return pl.pallas_call(
        near_kernel,
        in_specs=[IN_VMEM] * 4 + [ANYWHERE] * len(after),
        out_specs=[IN_VMEM] * 3,
        out_shape=[spec(shape, jnp.bfloat16)] * 2 + [spec((2 * modes, 2 * modes))],
        scratch_shapes=[pltpu.VMEM(shape, jnp.bfloat16)] * 2,
        cost_estimate=cost(1 << 20, 8 << 20),
        compiler_params=compiled(),
    )(*(a.reshape(-1, depth) for a in (stiff, own, by_x)), mass, *after)


def far_product(p, core_ref, both_ref, left_top, left_rest, top, rest):
    modes = top.shape[0] // 2
    first, second = pl.ds(0, modes), pl.ds(modes, modes)
    rows = top.shape[1] // (3 * both_ref.shape[1])

    def do(row, at):
        comp, inner = lax.div(row, rows), lax.rem(row, rows)
        core_row = (2 * comp + p) * rows + inner
        top[first, at], rest[first, at] = split(modes_at(core_ref, core_row, modes))
        top[second, at], rest[second, at] = split(modes_at(both_ref, row, modes))

    each_row(both_ref, modes, do)
    return product(top[...], rest[...], left_top[...], left_rest[...])


def far_kernel(p, core_ref, both_ref, left_top, left_rest, out_ref, top, rest):
    out_ref[...] = far_product(p, core_ref, both_ref, left_top, left_rest, top, rest)


def last_kernel(factor, p, core_ref, both_ref, left_top, left_rest, place_ref, *refs):
    nears, fars, out_ref, top, rest, turned = refs[:2], refs[2:-4], *refs[-4:]
    far = far_product(p, core_ref, both_ref, left_top, left_rest, top, rest)
    modes = top.shape[0] // 2
    far = far + fars[0][...]
    near = nears[0][...] + nears[1][...]
    blocks = (near[:modes], far[:modes], near[modes:], far[modes:])
    for r in range(4):
        at = pl.ds(pl.multiple_of(place_ref[r] * modes, modes), modes)
        turned[at, :] = blocks[r] * factor
    whole = turned[...].T
    out_ref[0 : 2 * modes, :] = whole[:, :128]
    tail = whole[:, 128:]
    out_ref[2 * modes :, :] = jnp.concatenate([tail[:modes], tail[modes:]], 1)


def far_gram(p, by_core, by_both, left, modes, last=None):
    wide = by_both.size // modes
    shape = (2 * modes, wide)
    depth = by_core.shape[-1]
    args = [a.reshape(-1, depth) for a in (by_core, by_both)] + list(left)
    specs = [IN_VMEM] * 4
    scratch = [pltpu.VMEM(shape, jnp.bfloat16)] * 2
    if last is None:
        kernel, out = partial(far_kernel, p), (2 * modes, 2 * modes)
    else:
        factor, place, nears, fars = last
        kernel, out = partial(last_kernel, factor, p), (3 * modes, 128)
        args += [place, *nears, *fars]
        specs += [pl.BlockSpec(memory_space=pltpu.SMEM)] + [IN_VMEM] * 3
        scratch.append(pltpu.VMEM((4 * modes, 2 * modes), jnp.float32))
    return pl.pallas_call(
        kernel,
        in_specs=specs,
        out_specs=IN_VMEM,
        out_shape=spec(out),
        scratch_shapes=scratch,
        cost_estimate=cost(1 << 20, 8 << 20),
        compiler_params=compiled(),
    )(*args)


def total_over(x, axes, groups):
    above, count, below = groups
    parts = []
    for k in range(1, count):
        pairs = [
            ((i * count + j) * below + l, (i * count + (j + k) % count) * below + l)
            for i in range(above)
            for j in range(count)
            for l in range(below)
        ]
        parts.append(lax.ppermute(x, axes, pairs))
    for part in parts:
        x = x + part
    return x


def body(subspace, modulus, mass, support, stiffness):
    modes, comps, planes, rows, depth = subspace.shape
    slabs = lax.axis_size(SLAB)
    four = lax.axis_size(MODE)
    up = [
        (i * four + m, (i + 1) * four + m if i + 1 < slabs else m ^ 2)
        for i in range(slabs)
        for m in range(four)
    ]
    down = [(b, a) for a, b in up]
    everywhere = SLAB + MODE
    *current, edge = start(
        subspace.reshape(modes * comps, planes, rows, depth), support, modulus
    )
    lower_layer = lax.ppermute(edge, everywhere, up)
    free = (1 - support).astype(jnp.float32)
    layers = jnp.concatenate([lower_layer, modulus], 0)
    plane_index = (
        lax.axis_index(SLAB) * planes - 1 + lax.broadcasted_iota(jnp.int32, layers.shape, 0)
    )
    row_index = lax.broadcasted_iota(jnp.int32, layers.shape, 1)
    depth_index = lax.broadcasted_iota(jnp.int32, layers.shape, 2)
    valid = (
        (plane_index >= 0)
        & (plane_index < planes * slabs - 1)
        & (row_index < rows - 1)
        & (depth_index < depth - 1)
    )
    layers = jnp.where(valid, layers, jnp.zeros_like(layers))
    own_coef, halo_coef = coefficients(stiffness, layers)
    scale = free / (mass * HALF)

    before = ()
    lower = lax.ppermute(current[1], everywhere, up)
    upper = lax.ppermute(current[0], everywhere, down)
    for k in range(4):
        times = 1.0 if k == 0 else 2.0
        part = own_part(times * CENTER / HALF, current, own_coef, times * scale, before)
        high = with_halo(1, upper, part[1], halo_coef, times * scale)
        below = lax.ppermute(high, everywhere, up)
        low = with_halo(0, lower, part[0], halo_coef, times * scale)
        upper = lax.ppermute(low, everywhere, down)
        lower = below
        before, current = current, (low, high)
    swap = [(0, 1), (1, 0)]
    by_x = [None, None]
    for p in (1, 0):
        by_x[p] = lax.ppermute(current[p], "xl", swap)
    filtered = joined(*current)
    part = own_part(0.0, current, own_coef, free, ())
    stiffened = [with_halo(p, h, part[p], halo_coef, free) for p, h in ((0, lower), (1, upper))]
    me = lax.axis_index(MODE)
    place = jnp.stack([me ^ r for r in range(4)]).astype(jnp.int32)
    factor = 1.0 / (float(comps) * planes * slabs * rows * depth)
    by_core = lax.ppermute(filtered, "core", swap)
    nears, fars = [], []
    after = (*stiffened, filtered)
    for p in (1, 0):
        by_x[p] = held(by_x[p], *after)
        by_both = lax.ppermute(by_x[p], "core", swap)
        *left, near = near_gram(
            stiffened[p], current[p], by_x[p], mass[p], modes, by_x[:1] if p else ()
        )
        nears.append(near)
        last = (factor, place, nears, fars) if p == 0 else None
        fars.append(far_gram(p, by_core, by_both, left, modes, last))
        after = (near,)
    grams = fars[-1]
    for groups in ((16, 4, 1), (8, 2, 4), (2, 4, 8), (1, 2, 32)):
        grams = total_over(grams, SLAB, groups)
    tail = grams[2 * modes :]
    wide = 4 * modes - depth
    stiffness_gram = jnp.concatenate([grams[:modes], tail[:, :wide]], 1)
    mass_gram = jnp.concatenate([grams[modes : 2 * modes], tail[:, wide:]], 1)
    return filtered.reshape(subspace.shape), stiffness_gram, mass_gram


def solution(mesh):
    finer = Mesh(mesh.devices.reshape(2, 8, 4, 2, 2), SLAB + MODE)
    placed = (
        P(MODE, None, SLAB, None, None),
        P(SLAB, None, None),
        P(SLAB, None, None),
        P(SLAB, None, None),
        P(),
    )
    return jax.shard_map(
        body,
        mesh=finer,
        in_specs=placed,
        out_specs=(P(MODE, None, SLAB, None, None), P(MODE, None), P(MODE, None)),
        check_vma=False,
    )
```

```python
from functools import partial

import jax
import jax.numpy as jnp
from jax import lax
from jax.experimental import pallas as pl
from jax.experimental.pallas import tpu as pltpu
from jax.sharding import Mesh, PartitionSpec as P

CENTER = 110.0
HALF = 90.0
SLAB = ("xh", "z", "y")
MODE = ("xl", "core")
STEPS = (0, 1, -1)
VMEM_LIMIT = 16 * 1024 * 1024


def spec(shape, dtype=jnp.float32):
    return jax.ShapeDtypeStruct(shape, dtype)


def own_index(dz, q, e, dy, c, p):
    return ((((STEPS.index(dz) * 2 + q) * 3 + e) * 3 + STEPS.index(dy)) * 3 + c) * 2 + p


def halo_index(dz, side, e, dy, c):
    return (((STEPS.index(dz) * 2 + side) * 3 + e) * 3 + STEPS.index(dy)) * 3 + c


def rolled(x, by, axis):
    by = by % x.shape[axis]
    return x if by == 0 else pltpu.roll(x, by, axis)


def coefficient_kernel(stiff_ref, layers_ref, own_ref, halo_ref):
    turned = {}
    for layer in range(3):
        for b in range(2):
            for d in range(2):
                turned[layer, b, d] = rolled(rolled(layers_ref[layer], b, 0), d, 1)
    for p in range(2):
        for q in range(-1, 3):
            dx = q - p
            if abs(dx) > 1:
                continue
            for dy in STEPS:
                for dz in STEPS:
                    corners = [
                        (a, b, d)
                        for a in range(2)
                        for b in range(2)
                        for d in range(2)
                        if 0 <= a + dx <= 1 and 0 <= b + dy <= 1 and 0 <= d + dz <= 1
                    ]
                    for c in range(3):
                        for e in range(3):
                            total = None
                            for a, b, d in corners:
                                row = 3 * (4 * a + 2 * b + d) + c
                                col = 3 * (4 * (a + dx) + 2 * (b + dy) + d + dz) + e
                                term = stiff_ref[row, col] * turned[p - a + 1, b + dy, d]
                                total = term if total is None else total + term
                            if 0 <= q <= 1:
                                own_ref[own_index(dz, q, e, dy, c, p)] = total
                            else:
                                halo_ref[halo_index(dz, 0 if q < 0 else 1, e, dy, c)] = total


def coefficients(stiffness, layers):
    rows, depth = layers.shape[1:]
    return pl.pallas_call(
        coefficient_kernel,
        in_specs=[pl.BlockSpec(memory_space=pltpu.SMEM), pl.BlockSpec(memory_space=pltpu.VMEM)],
        out_specs=[pl.BlockSpec(memory_space=pltpu.VMEM)] * 2,
        out_shape=[spec((324, rows, depth)), spec((162, rows, depth))],
        compiler_params=pltpu.CompilerParams(vmem_limit_bytes=VMEM_LIMIT),
    )(stiffness, layers)


OWN_MODES = 2
HALO_MODES = 4
IN_VMEM = pl.BlockSpec(memory_space=pltpu.VMEM)
ANYWHERE = pl.BlockSpec(memory_space=pl.ANY)


def cost(flops, nbytes):
    return pl.CostEstimate(flops=flops, bytes_accessed=nbytes, transcendentals=0)


def compiled():
    return pltpu.CompilerParams(vmem_limit_bytes=VMEM_LIMIT)


def gathered(acc):
    return acc[0] + rolled(acc[1], -1, 0) + rolled(acc[2], 1, 0)


def start_kernel(field_ref, support_ref, modulus_ref, low_ref, high_ref, edge_ref):
    free = [(1 - support_ref[p]).astype(jnp.float32) for p in range(2)]
    low_ref[...] = field_ref[:, 0] * free[0]
    high_ref[...] = field_ref[:, 1] * free[1]
    edge_ref[0] = modulus_ref[1]


def start(field, support, modulus):
    count, planes, rows, depth = field.shape
    tile = count // 4
    plane = pl.BlockSpec((tile, rows, depth), lambda i: (i, 0, 0))
    edge = pl.BlockSpec((1, rows, depth), lambda i: (0, 0, 0))
    both = pl.BlockSpec((planes, rows, depth), lambda i: (0, 0, 0))
    return pl.pallas_call(
        start_kernel,
        grid=(4,),
        in_specs=[pl.BlockSpec((tile, planes, rows, depth), lambda i: (i, 0, 0, 0)), both, both],
        out_specs=[plane, plane, edge],
        out_shape=[spec((count, rows, depth))] * 2 + [spec((1, rows, depth))],
        cost_estimate=cost(2 * field.size, 8 * field.size),
        compiler_params=compiled(),
    )(field, support, modulus)


def added(acc, key, term):
    acc[key] = acc[key] + term if key in acc else term


def own_kernel(shift, count, *refs):
    low_ref, high_ref, coef_ref, scale_ref = refs[:4]
    before, parts = refs[4:-2], refs[-2:]
    planes = (low_ref, high_ref)

    def some(i, _):
        base = i * (3 * OWN_MODES)
        acc = {}
        for dz in STEPS:
            for q in range(2):
                for e in range(3):
                    fields = [rolled(planes[q][base + 3 * u + e], -dz, 1) for u in range(OWN_MODES)]
                    for s, dy in enumerate(STEPS):
                        for c in range(3):
                            for p in range(2):
                                coef = coef_ref[own_index(dz, q, e, dy, c, p)]
                                for u in range(OWN_MODES):
                                    added(acc, (u, c, p, s), coef * fields[u])
        for u in range(OWN_MODES):
            for c in range(3):
                at = base + 3 * u + c
                for p in range(2):
                    value = scale_ref[p] * gathered([acc[u, c, p, s] for s in range(3)])
                    if shift:
                        value = value - shift * planes[p][at]
                    if before:
                        value = value - before[p][at]
                    parts[p][at] = value
        return 0

    lax.fori_loop(0, count // (3 * OWN_MODES), some, 0)


def own_part(shift, current, coef, scale, before):
    count, rows, depth = current[0].shape
    args = (*current, coef, scale, *before)
    return pl.pallas_call(
        partial(own_kernel, shift, count),
        in_specs=[IN_VMEM] * len(args),
        out_specs=[IN_VMEM] * 2,
        out_shape=[spec(current[0].shape)] * 2,
        cost_estimate=cost(2 * 108 * count * rows * depth, 16 << 20),
        compiler_params=compiled(),
    )(*args)


def halo_kernel(p, halo_ref, part_ref, coef_ref, scale_ref, out_ref):
    step = 3 * HALO_MODES

    def some(i, _):
        base = i * step
        acc = {}
        for dz in STEPS:
            for e in range(3):
                fields = [rolled(halo_ref[base + 3 * u + e], -dz, 1) for u in range(HALO_MODES)]
                for s, dy in enumerate(STEPS):
                    for c in range(3):
                        coef = coef_ref[halo_index(dz, p, e, dy, c)]
                        for u in range(HALO_MODES):
                            added(acc, (u, c, s), coef * fields[u])
        scale = scale_ref[p]
        for u in range(HALO_MODES):
            for c in range(3):
                at = base + 3 * u + c
                out_ref[at] = part_ref[at] + scale * gathered([acc[u, c, s] for s in range(3)])
        return 0

    lax.fori_loop(0, halo_ref.shape[0] // step, some, 0)


def with_halo(p, halo, part, coef, scale):
    return pl.pallas_call(
        partial(halo_kernel, p),
        in_specs=[IN_VMEM] * 4,
        out_specs=IN_VMEM,
        out_shape=spec(halo.shape),
        cost_estimate=cost(54 * halo.size, 5 << 20),
        compiler_params=compiled(),
    )(halo, part, coef, scale)


def join_kernel(low_ref, high_ref, out_ref):
    def some(i, _):
        out_ref[i, 0] = low_ref[i]
        out_ref[i, 1] = high_ref[i]
        return 0

    lax.fori_loop(0, low_ref.shape[0], some, 0, unroll=8)


def joined(low, high):
    return pl.pallas_call(
        join_kernel,
        in_specs=[IN_VMEM] * 2,
        out_specs=IN_VMEM,
        out_shape=spec((low.shape[0], 2) + low.shape[1:]),
        cost_estimate=cost(1 << 20, 4 << 20),
        compiler_params=compiled(),
    )(low, high)


def split(x):
    top = x.astype(jnp.bfloat16)
    return top, (x - top.astype(jnp.float32)).astype(jnp.bfloat16)


def dot_t(a, b):
    return lax.dot_general(a, b, (((1,), (1,)), ((), ())), preferred_element_type=jnp.float32)


def product(top, rest, left_top, left_rest):
    return dot_t(top, left_top) + dot_t(rest, left_top) + dot_t(top, left_rest)


def each_row(field_ref, modes, do):
    stride, depth = field_ref.shape[0] // modes, field_ref.shape[1]

    def some(row, _):
        do(row, pl.ds(pl.multiple_of(row * depth, depth), depth))
        return 0

    lax.fori_loop(0, stride, some, 0, unroll=12)


def modes_at(ref, row, modes):
    return ref[pl.ds(row, modes, stride=ref.shape[0] // modes), :]


def held(x, *after):
    return pl.pallas_call(
        lambda *refs: None,
        in_specs=[ANYWHERE] * (1 + len(after)),
        out_specs=ANYWHERE,
        out_shape=spec(x.shape),
        input_output_aliases={0: 0},
        cost_estimate=cost(0, 1 << 10),
        compiler_params=compiled(),
    )(x, *after)


def near_kernel(stiff_ref, own_ref, field_ref, mass_ref, *refs):
    left_top, left_rest, out_ref, top, rest = refs[-5:]
    modes = top.shape[0] // 2
    first, second = pl.ds(0, modes), pl.ds(modes, modes)

    def do(row, at):
        own = modes_at(own_ref, row, modes)
        weight = mass_ref[pl.ds(lax.rem(row, mass_ref.shape[0]), 1), :]
        left_top[first, at], left_rest[first, at] = split(modes_at(stiff_ref, row, modes))
        left_top[second, at], left_rest[second, at] = split(own * weight)
        top[first, at], rest[first, at] = split(own)
        top[second, at], rest[second, at] = split(modes_at(field_ref, row, modes))

    each_row(own_ref, modes, do)
    out_ref[...] = product(top[...], rest[...], left_top[...], left_rest[...])


def near_gram(stiff, own, by_x, mass, modes, after=()):
    wide = own.size // modes
    shape = (2 * modes, wide)
    depth = mass.shape[-1]
    return pl.pallas_call(
        near_kernel,
        in_specs=[IN_VMEM] * 4 + [ANYWHERE] * len(after),
        out_specs=[IN_VMEM] * 3,
        out_shape=[spec(shape, jnp.bfloat16)] * 2 + [spec((2 * modes, 2 * modes))],
        scratch_shapes=[pltpu.VMEM(shape, jnp.bfloat16)] * 2,
        cost_estimate=cost(1 << 20, 8 << 20),
        compiler_params=compiled(),
    )(*(a.reshape(-1, depth) for a in (stiff, own, by_x)), mass, *after)


def far_product(p, core_ref, both_ref, left_top, left_rest, top, rest):
    modes = top.shape[0] // 2
    first, second = pl.ds(0, modes), pl.ds(modes, modes)
    rows = top.shape[1] // (3 * both_ref.shape[1])

    def do(row, at):
        comp, inner = lax.div(row, rows), lax.rem(row, rows)
        core_row = (2 * comp + p) * rows + inner
        top[first, at], rest[first, at] = split(modes_at(core_ref, core_row, modes))
        top[second, at], rest[second, at] = split(modes_at(both_ref, row, modes))

    each_row(both_ref, modes, do)
    return product(top[...], rest[...], left_top[...], left_rest[...])


def far_kernel(p, core_ref, both_ref, left_top, left_rest, out_ref, top, rest):
    out_ref[...] = far_product(p, core_ref, both_ref, left_top, left_rest, top, rest)


def last_kernel(factor, p, core_ref, both_ref, left_top, left_rest, place_ref, *refs):
    nears, fars, out_ref, top, rest, turned = refs[:2], refs[2:-4], *refs[-4:]
    far = far_product(p, core_ref, both_ref, left_top, left_rest, top, rest)
    modes = top.shape[0] // 2
    far = far + fars[0][...]
    near = nears[0][...] + nears[1][...]
    blocks = (near[:modes], far[:modes], near[modes:], far[modes:])
    for r in range(4):
        at = pl.ds(pl.multiple_of(place_ref[r] * modes, modes), modes)
        turned[at, :] = blocks[r] * factor
    whole = turned[...].T
    out_ref[0 : 2 * modes, :] = whole[:, :128]
    tail = whole[:, 128:]
    out_ref[2 * modes :, :] = jnp.concatenate([tail[:modes], tail[modes:]], 1)


def far_gram(p, by_core, by_both, left, modes, last=None):
    wide = by_both.size // modes
    shape = (2 * modes, wide)
    depth = by_core.shape[-1]
    args = [a.reshape(-1, depth) for a in (by_core, by_both)] + list(left)
    specs = [IN_VMEM] * 4
    scratch = [pltpu.VMEM(shape, jnp.bfloat16)] * 2
    if last is None:
        kernel, out = partial(far_kernel, p), (2 * modes, 2 * modes)
    else:
        factor, place, nears, fars = last
        kernel, out = partial(last_kernel, factor, p), (3 * modes, 128)
        args += [place, *nears, *fars]
        specs += [pl.BlockSpec(memory_space=pltpu.SMEM)] + [IN_VMEM] * 3
        scratch.append(pltpu.VMEM((4 * modes, 2 * modes), jnp.float32))
    return pl.pallas_call(
        kernel,
        in_specs=specs,
        out_specs=IN_VMEM,
        out_shape=spec(out),
        scratch_shapes=scratch,
        cost_estimate=cost(1 << 20, 8 << 20),
        compiler_params=compiled(),
    )(*args)


def total_over(x, axes, groups):
    above, count, below = groups
    parts = []
    for k in range(1, count):
        pairs = [
            ((i * count + j) * below + l, (i * count + (j + k) % count) * below + l)
            for i in range(above)
            for j in range(count)
            for l in range(below)
        ]
        parts.append(lax.ppermute(x, axes, pairs))
    for part in parts:
        x = x + part
    return x


def body(subspace, modulus, mass, support, stiffness):
    modes, comps, planes, rows, depth = subspace.shape
    slabs = lax.axis_size(SLAB)
    four = lax.axis_size(MODE)
    up = [
        (i * four + m, (i + 1) * four + m if i + 1 < slabs else m ^ 2)
        for i in range(slabs)
        for m in range(four)
    ]
    down = [(b, a) for a, b in up]
    everywhere = SLAB + MODE
    *current, edge = start(
        subspace.reshape(modes * comps, planes, rows, depth), support, modulus
    )
    lower_layer = lax.ppermute(edge, everywhere, up)
    free = (1 - support).astype(jnp.float32)
    layers = jnp.concatenate([lower_layer, modulus], 0)
    plane_index = (
        lax.axis_index(SLAB) * planes - 1 + lax.broadcasted_iota(jnp.int32, layers.shape, 0)
    )
    row_index = lax.broadcasted_iota(jnp.int32, layers.shape, 1)
    depth_index = lax.broadcasted_iota(jnp.int32, layers.shape, 2)
    valid = (
        (plane_index >= 0)
        & (plane_index < planes * slabs - 1)
        & (row_index < rows - 1)
        & (depth_index < depth - 1)
    )
    layers = jnp.where(valid, layers, jnp.zeros_like(layers))
    own_coef, halo_coef = coefficients(stiffness, layers)
    scale = free / (mass * HALF)

    before = ()
    lower = lax.ppermute(current[1], everywhere, up)
    upper = lax.ppermute(current[0], everywhere, down)
    for k in range(4):
        times = 1.0 if k == 0 else 2.0
        part = own_part(times * CENTER / HALF, current, own_coef, times * scale, before)
        high = with_halo(1, upper, part[1], halo_coef, times * scale)
        below = lax.ppermute(high, everywhere, up)
        low = with_halo(0, lower, part[0], halo_coef, times * scale)
        upper = lax.ppermute(low, everywhere, down)
        lower = below
        before, current = current, (low, high)
    swap = [(0, 1), (1, 0)]
    by_x = [None, None]
    for p in (1, 0):
        by_x[p] = lax.ppermute(current[p], "xl", swap)
    filtered = joined(*current)
    part = own_part(0.0, current, own_coef, free, ())
    stiffened = [with_halo(p, h, part[p], halo_coef, free) for p, h in ((0, lower), (1, upper))]
    me = lax.axis_index(MODE)
    place = jnp.stack([me ^ r for r in range(4)]).astype(jnp.int32)
    factor = 1.0 / (float(comps) * planes * slabs * rows * depth)
    by_core = lax.ppermute(filtered, "core", swap)
    nears, fars = [], []
    after = (*stiffened, filtered)
    for p in (1, 0):
        by_x[p] = held(by_x[p], *after)
        by_both = lax.ppermute(by_x[p], "core", swap)
        *left, near = near_gram(
            stiffened[p], current[p], by_x[p], mass[p], modes, by_x[:1] if p else ()
        )
        nears.append(near)
        last = (factor, place, nears, fars) if p == 0 else None
        fars.append(far_gram(p, by_core, by_both, left, modes, last))
        after = (near, fars[0])
    grams = fars[-1]
    for groups in ((16, 4, 1), (8, 2, 4), (2, 4, 8), (1, 2, 32)):
        grams = total_over(grams, SLAB, groups)
    tail = grams[2 * modes :]
    wide = 4 * modes - depth
    stiffness_gram = jnp.concatenate([grams[:modes], tail[:, :wide]], 1)
    mass_gram = jnp.concatenate([grams[modes : 2 * modes], tail[:, wide:]], 1)
    return filtered.reshape(subspace.shape), stiffness_gram, mass_gram


def solution(mesh):
    finer = Mesh(mesh.devices.reshape(2, 8, 4, 2, 2), SLAB + MODE)
    placed = (
        P(MODE, None, SLAB, None, None),
        P(SLAB, None, None),
        P(SLAB, None, None),
        P(SLAB, None, None),
        P(),
    )
    return jax.shard_map(
        body,
        mesh=finer,
        in_specs=placed,
        out_specs=(P(MODE, None, SLAB, None, None), P(MODE, None), P(MODE, None)),
        check_vma=False,
    )
```
